32 devices in a mesh: seq: 8 (over y, x, core), head: 4 (over z).
Axes of the slice: x: 2, y: 2, z: 4, core: 2. Of those that a mesh axis runs over, the one named last changes fastest.
Arguments:
- queries: bfloat16 [4096, 512], P('seq', 'head'), may hold values from -6 to 6
- key_rows: bfloat16 [4096, 512], P('seq', 'head'), may hold values from -6 to 6
- value_rows: bfloat16 [4096, 512], P('seq', 'head'), may hold values from -6 to 6
- upstream: bfloat16 [4096, 512], P('seq', 'head'), may hold values from -6 to 6
- exit_weight: bfloat16 [512], P('head'), may hold values from -4 to 4
- labels: int32 [4096], P('seq'), may hold values 0 or 1
- rand_blocks: int32 [64, 3], replicated, may hold values from 0 to 63, as said below
- glob_blocks: int32 [2], replicated, may hold values from 0 to 63, as said below
Outputs:
- attended: bfloat16 [4096, 512], P('seq', 'head')
- token_loss: float32 [4096], P('seq')
- grad_query: float32 [4096, 512], P('seq', 'head')
- grad_key: float32 [4096, 512], P('seq', 'head')
- grad_value: float32 [4096, 512], P('seq', 'head')
The draws below stay inside these ranges and needn't reach their ends.
Inputs may be any that keep to these rules, and one draw needn't show every extreme that they name: `rand_blocks`: among the 24 entries of the rows of one device (aligned groups of 8 rows), at most 3 lie in any one aligned range of 8 key blocks, and some range holds exactly 3. `glob_blocks`: 2 distinct blocks, the same for every query block; the document's last block is always among them.
All inputs are finite; a program needn't handle non-finite values. No bound on the sum of `labels` on one device may be relied on, other than what follows from the above.
Results may differ from the reference program's by a relative error of at most 0.018.
Values may be sent and summed in bfloat16 or wider, within the bound.
A program may use at most 64 MiB of HBM per device.

```python
import math
import jax
import jax.numpy as jnp
from jax import lax

HEAD_SIZE = 128
BLOCK = 64
RAND = 3
GLOBAL = 2
BPD = 8
HEADS = 4
SLOTS = 8
DOC_TOKENS = 4096
NBLOCKS = 64
RAND_DEV = 24
CAP_R = 3


def qk_pair(key):
    columns = HEADS * HEAD_SIZE
    queries = jnp.clip(jax.random.normal(jax.random.fold_in(key, 21), (DOC_TOKENS, columns), jnp.float32), -6.0, 6.0)
    key_vals = jnp.clip(jax.random.normal(jax.random.fold_in(key, 22), (DOC_TOKENS, columns), jnp.float32), -6.0, 6.0)
    return (queries, key_vals)


def draw_queries(key, part):
    return qk_pair(key)[0].astype(jnp.bfloat16)


def draw_key_rows(key, part):
    return qk_pair(key)[1].astype(jnp.bfloat16)


def draw_exit_weight(key, part):
    columns = HEADS * HEAD_SIZE
    ramp = (jnp.arange(columns) // HEAD_SIZE).astype(jnp.float32) / max(HEADS - 1, 1)
    values = 0.2 * (1.0 + 2.0 * ramp) * jnp.clip(jax.random.normal(jax.random.fold_in(key, 32), (columns,), jnp.float32), -6.0, 6.0)
    return values.astype(jnp.bfloat16)


def draw_rand_blocks(key, part):
    shards = NBLOCKS // BPD
    busy_owner = jax.random.randint(jax.random.fold_in(key, 7), (), 0, shards)

    def device_draw(device):
        dev_key = jax.random.fold_in(key, 1000 + device)
        spread = jax.random.permutation(jax.random.fold_in(dev_key, 1), (shards - 1) * CAP_R)[:RAND_DEV - CAP_R]
        others = (busy_owner + 1 + spread // CAP_R) % shards
        owners = jnp.concatenate([jnp.zeros((CAP_R,), jnp.int32) + busy_owner, others.astype(jnp.int32)])
        owners = owners[jax.random.permutation(jax.random.fold_in(dev_key, 2), RAND_DEV)]
        offsets = jax.random.randint(jax.random.fold_in(dev_key, 3), (RAND_DEV,), 0, BPD)
        return (owners * BPD + offsets).astype(jnp.int32).reshape(BPD, RAND)
    return jax.vmap(device_draw)(jnp.arange(shards)).reshape(NBLOCKS, RAND).astype(jnp.int32)


def draw_glob_blocks(key, part):
    others = jax.random.permutation(jax.random.fold_in(key, 5), NBLOCKS - 1)[:GLOBAL - 1].astype(jnp.int32)
    chosen = jnp.concatenate([others, jnp.zeros((1,), jnp.int32) + (NBLOCKS - 1)])
    order = jax.random.permutation(jax.random.fold_in(key, 6), GLOBAL)
    return chosen[order].astype(jnp.int32)


def place_ends(values, own_key, smallest, high):
    index_at = [jax.random.randint(jax.random.fold_in(own_key, axis), (), 0, length) for axis, length in enumerate(values.shape)]
    main_axis = values.shape.index(max(values.shape))
    neighbour = index_at[:main_axis] + [(index_at[main_axis] + 1) % values.shape[main_axis]] + index_at[main_axis + 1:]
    return values.at[tuple(index_at)].set(smallest).at[tuple(neighbour)].set(high)


def shard_levels(own_key, extent, cuts, least, high):
    gain = 1.0
    for position, parts in cuts:
        steps = jax.random.uniform(jax.random.fold_in(jax.random.fold_in(own_key, 6), position), (parts,), jnp.float32, least / len(cuts), high / len(cuts))
        gain = gain * jnp.repeat(jnp.exp(steps), extent[position] // parts).reshape((-1,) + (1,) * (len(extent) - 1 - position))
    return gain


def normal_values(own_key, shape, deviation, reach, cuts=(), kind=jnp.bfloat16):
    entries = deviation * jax.random.normal(own_key, shape, jnp.float32)
    if cuts:
        entries = entries * shard_levels(own_key, shape, cuts, -0.22, 0.18)
    return jnp.clip(entries, -reach, reach).astype(kind)


def setup_inputs(seed: int = 0) -> dict:
    arg_keys = jax.random.split(jax.random.key(seed), 9)
    return {
        "queries": draw_queries(jax.random.fold_in(arg_keys[8], 71), 0),
        "key_rows": draw_key_rows(jax.random.fold_in(arg_keys[8], 71), 0),
        "value_rows": normal_values(arg_keys[2], (DOC_TOKENS, HEADS * HEAD_SIZE), 1.0, 6.0, ((0, 8), (1, 4))),
        "upstream": normal_values(arg_keys[3], (DOC_TOKENS, HEADS * HEAD_SIZE), 1.0, 6.0, ((0, 8), (1, 4))),
        "exit_weight": draw_exit_weight(jax.random.fold_in(arg_keys[8], 71), 0),
        "labels": place_ends((jax.random.randint(arg_keys[5], (DOC_TOKENS,), 0, 2) < 1).astype(jnp.int32), jax.random.fold_in(arg_keys[5], 1), 0, 1),
        "rand_blocks": draw_rand_blocks(jax.random.fold_in(arg_keys[8], 71), 0),
        "glob_blocks": draw_glob_blocks(jax.random.fold_in(arg_keys[8], 71), 0),
    }


def build_keys(kv_blocks, rand_blocks, glob_blocks):
    prev_blocks = jnp.roll(kv_blocks, 1, axis=0)
    next_blocks = jnp.roll(kv_blocks, -1, axis=0)
    random_part = kv_blocks[rand_blocks]
    global_part = jnp.broadcast_to(kv_blocks[glob_blocks][None], (NBLOCKS, GLOBAL, BLOCK, 2 * HEAD_SIZE))
    gathered_keys = jnp.concatenate([prev_blocks[:, None], kv_blocks[:, None], next_blocks[:, None], random_part, global_part], axis=1)
    return gathered_keys.reshape(NBLOCKS, SLOTS * BLOCK, 2 * HEAD_SIZE)

def key_valid():
    block_ids = jnp.arange(NBLOCKS)
    slot_ok = jnp.concatenate([(block_ids > 0)[:, None], jnp.ones((NBLOCKS, 1), bool), (block_ids < NBLOCKS - 1)[:, None], jnp.ones((NBLOCKS, RAND + GLOBAL), bool)], axis=1)
    return jnp.repeat(slot_ok, BLOCK, axis=1)

def attention_probs(head_q, gathered_keys):
    blocked_queries = head_q.reshape(NBLOCKS, BLOCK, HEAD_SIZE).astype(jnp.float32)
    attention_scores = jnp.einsum('afs,ans->afn', blocked_queries, gathered_keys[..., :HEAD_SIZE].astype(jnp.float32)) / math.sqrt(HEAD_SIZE)
    attention_scores = jnp.where(key_valid()[:, None, :], attention_scores, -jnp.inf)
    row_peak = lax.optimization_barrier(jnp.max(attention_scores, axis=-1, keepdims=True))
    exp_terms = jnp.exp(attention_scores - row_peak)
    return exp_terms / lax.optimization_barrier(jnp.sum(exp_terms, axis=-1, keepdims=True))

def round_low(values):
    return lax.optimization_barrier(values.astype(jnp.bfloat16)).astype(jnp.float32)

def reference(queries, key_rows, value_rows, upstream, exit_weight, labels, rand_blocks, glob_blocks):

    def split_heads(values):
        return values.reshape(DOC_TOKENS, HEADS, HEAD_SIZE).transpose(1, 0, 2)
    q_heads = split_heads(queries)
    kv_heads = jnp.concatenate([split_heads(key_rows), split_heads(value_rows)], axis=-1)

    def forward_one(inputs):
        head_q, head_kv = inputs
        gathered_keys = build_keys(head_kv.reshape(NBLOCKS, BLOCK, 2 * HEAD_SIZE), rand_blocks, glob_blocks)
        reduced_probabilities = attention_probs(head_q, gathered_keys).astype(jnp.bfloat16)
        head_output = jnp.einsum('omc,och->omh', reduced_probabilities.astype(jnp.float32), gathered_keys[..., HEAD_SIZE:].astype(jnp.float32))
        return head_output.astype(jnp.bfloat16).reshape(DOC_TOKENS, HEAD_SIZE)
    heads_out = lax.map(forward_one, (q_heads, kv_heads))
    attended = heads_out.transpose(1, 0, 2).reshape(DOC_TOKENS, HEADS * HEAD_SIZE)
    logits = jnp.dot(attended, exit_weight, preferred_element_type=jnp.float32)
    target = labels.astype(jnp.float32)
    token_loss = jax.nn.softplus(logits) - target * logits
    dlogits = jax.nn.sigmoid(logits) - target
    grad_out = (upstream.astype(jnp.float32) + dlogits[:, None] * exit_weight.astype(jnp.float32)[None, :]).astype(jnp.bfloat16)
    g_heads = split_heads(grad_out)

    def backward_one(inputs):
        head_q, head_kv, head_g = inputs
        gathered_keys = build_keys(head_kv.reshape(NBLOCKS, BLOCK, 2 * HEAD_SIZE), rand_blocks, glob_blocks)
        probs = attention_probs(head_q, gathered_keys)
        reduced_probabilities = probs.astype(jnp.bfloat16).astype(jnp.float32)
        key_portion = gathered_keys[..., :HEAD_SIZE].astype(jnp.float32)
        value_portion = gathered_keys[..., HEAD_SIZE:].astype(jnp.float32)
        block_gradient = head_g.reshape(NBLOCKS, BLOCK, HEAD_SIZE).astype(jnp.float32)
        blocked_queries = head_q.reshape(NBLOCKS, BLOCK, HEAD_SIZE).astype(jnp.float32)
        probability_gradient = jnp.einsum('afs,ans->afn', block_gradient, value_portion)
        row_dot = lax.optimization_barrier(jnp.sum(probs * probability_gradient, axis=-1, keepdims=True))
        score_gradient = (probs * (probability_gradient - row_dot) / math.sqrt(HEAD_SIZE)).astype(jnp.bfloat16).astype(jnp.float32)
        head_query_gradient = jnp.einsum('omc,och->omh', score_gradient, key_portion).reshape(DOC_TOKENS, HEAD_SIZE)
        key_gradient = jnp.einsum('tnc,tny->tcy', score_gradient, blocked_queries)
        value_gradient = jnp.einsum('tnc,tny->tcy', reduced_probabilities, block_gradient)
        slot_grads = jnp.concatenate([key_gradient, value_gradient], axis=-1).reshape(NBLOCKS, SLOTS, BLOCK, 2 * HEAD_SIZE)
        to_prev = round_low(slot_grads[:, 0])
        to_next = round_low(slot_grads[:, 2])
        rand_grads = round_low(slot_grads[:, 3:3 + RAND])
        zero_block = jnp.zeros((1, BLOCK, 2 * HEAD_SIZE), jnp.float32)
        kv_total = slot_grads[:, 1] + jnp.concatenate([to_prev[1:], zero_block], axis=0) + jnp.concatenate([zero_block, to_next[:-1]], axis=0)
        kv_total = kv_total.at[rand_blocks.reshape(-1)].add(rand_grads.reshape(NBLOCKS * RAND, BLOCK, 2 * HEAD_SIZE))
        kv_total = kv_total.at[glob_blocks].add(lax.optimization_barrier(jnp.sum(slot_grads[:, 3 + RAND:], axis=0)))
        return (head_query_gradient, kv_total.reshape(DOC_TOKENS, 2 * HEAD_SIZE))
    dq_heads, dkv_heads = lax.map(backward_one, (q_heads, kv_heads, g_heads))
    grad_query = dq_heads.transpose(1, 0, 2).reshape(DOC_TOKENS, HEADS * HEAD_SIZE)
    grad_key = dkv_heads[..., :HEAD_SIZE].transpose(1, 0, 2).reshape(DOC_TOKENS, HEADS * HEAD_SIZE)
    grad_value = dkv_heads[..., HEAD_SIZE:].transpose(1, 0, 2).reshape(DOC_TOKENS, HEADS * HEAD_SIZE)
    return (attended, token_loss, grad_query, grad_key, grad_value)
```

```python
import functools
import math

import jax
import jax.numpy as jnp
from jax import lax
from jax.experimental import pallas as pl
from jax.experimental.pallas import tpu as pltpu
from jax.sharding import PartitionSpec as P

BLOCK = 64
RAND = 3
GLOBAL = 2
SLOTS = 3 + RAND + GLOBAL
MESH = pl.DeviceIdType.MESH
F32 = jnp.float32
BF16 = jnp.bfloat16
CONTRACT_LAST = (((1,), (1,)), ((), ()))
CONTRACT_FIRST = (((0,), (0,)), ((), ()))
PARTS = 8


def flip(me, bits):
    out = me
    bit = 1
    while bit <= bits:
        if bits & bit:
            out = out + (1 - 2 * lax.rem(lax.div(me, jnp.int32(bit)), jnp.int32(2))) * bit
        bit *= 2
    return out


def kernel(
    S, H, nb, D, cap,
    q_ref, k_ref, v_ref, up_ref, w_ref, lab_ref, rand_ref, glob_ref,
    att_ref, loss_ref, dq_ref, dk_ref, dv_ref,
    kall, vall, p_s, ds_s, g_s, rg, og, og_in, acc, gacc, gsend, grecv, gsum, gall,
    edge_out, edge_in, lmine, lrecv, sidx, roff,
    ag_send, ag_fwd, ag_recv, l_send, l_recv, o_send, o_recv, e_send, e_recv,
    gp_send, gp_recv, gb_send, gb_recv,
):
    me = lax.axis_index("seq")
    hd = lax.axis_index("head")
    N = S * nb
    inv = 1.0 / math.sqrt(D)
    stride = max(1, S // PARTS)
    rows = GLOBAL * BLOCK // PARTS
    T = nb * BLOCK

    def seq_copy(src, dst, ssem, rsem, peer):
        return pltpu.make_async_remote_copy(
            src_ref=src, dst_ref=dst, send_sem=ssem, recv_sem=rsem,
            device_id={"seq": peer}, device_id_type=MESH)

    barrier = pltpu.get_barrier_semaphore()
    for d in range(1, S):
        pl.semaphore_signal(barrier, inc=1, device_id={"seq": flip(me, d)}, device_id_type=MESH)
    for d in range(1, H):
        pl.semaphore_signal(barrier, inc=1, device_id={"head": lax.rem(hd + d, H)}, device_id_type=MESH)
    pl.semaphore_wait(barrier, S - 1 + H - 1)

    mine = pl.ds(me * nb, nb)
    pairs = ((k_ref, kall), (v_ref, vall))
    evens = [d for d in range(S - 2, 0, -2)]
    partner = flip(me, 1)
    for a, (src, dst) in enumerate(pairs):
        for d in evens + [1]:
            seq_copy(src, dst.at[mine], ag_send.at[a, d], ag_recv.at[a, me], flip(me, d)).start()

    kall[mine] = k_ref[...]
    vall[mine] = v_ref[...]

    def tables(s, carry):
        zero = jnp.int32(0)
        cnt, cnt2 = zero, zero
        idx = [zero] * cap
        off = [jnp.int32(-1)] * cap
        for j in range(nb * RAND):
            b = rand_ref[me * nb + j // RAND, j % RAND]
            hit = lax.div(b, jnp.int32(nb)) == s
            c = rand_ref[s * nb + j // RAND, j % RAND]
            hit2 = lax.div(c, jnp.int32(nb)) == me
            place = lax.rem(c, jnp.int32(nb))
            for t in range(cap):
                idx[t] = jnp.where(hit & (cnt == t), j, idx[t])
                off[t] = jnp.where(hit2 & (cnt2 == t), place, off[t])
            cnt = cnt + hit.astype(jnp.int32)
            cnt2 = cnt2 + hit2.astype(jnp.int32)
        for t in range(cap):
            sidx[s, t] = idx[t]
            roff[s, t] = off[t]
        return carry

    lax.fori_loop(0, S, tables, 0)

    for a, (src, dst) in enumerate(pairs):
        for d in sorted(evens, key=lambda d: bin(d).count("1")):
            owner = flip(me, d)
            part = dst.at[pl.ds(owner * nb, nb)]
            seq_copy(src, part, ag_send.at[a, d], ag_recv.at[a, owner], owner).wait_recv()
            seq_copy(part, part, ag_fwd.at[a, d], ag_recv.at[a, owner], partner).start()
    for a, (src, dst) in enumerate(pairs):
        for d in range(1, S, 2):
            owner = flip(me, d)
            part = dst.at[pl.ds(owner * nb, nb)]
            seq_copy(src, part, ag_send.at[a, d], ag_recv.at[a, owner], owner).wait_recv()

    def gather(all_ref, i):
        gi = me * nb + i
        ids = [lax.rem(gi + N - 1, N), gi, lax.rem(gi + 1, N)]
        ids += [rand_ref[gi, r] for r in range(RAND)]
        ids += [glob_ref[r] for r in range(GLOBAL)]
        return jnp.concatenate([all_ref[b] for b in ids], axis=0)

    col = lax.broadcasted_iota(jnp.int32, (BLOCK, SLOTS * BLOCK), 1)

    def forward(i):
        keys = gather(kall, i)
        s = lax.dot_general(q_ref[i], keys, CONTRACT_LAST, preferred_element_type=F32) * inv
        gi = me * nb + i
        low = jnp.where(gi == 0, BLOCK, 0)
        void = (col < low) | ((col >= 2 * BLOCK) & (col < jnp.where(gi == N - 1, 3 * BLOCK, 0)))
        s = jnp.where(void, -jnp.inf, s)
        e = jnp.exp(s - jnp.max(s, axis=-1, keepdims=True))
        p = e * (1.0 / jnp.sum(e, axis=-1, keepdims=True))
        p_s[i] = p
        o = jnp.dot(p.astype(BF16), gather(vall, i), preferred_element_type=F32)
        att_ref[i] = o.astype(BF16)

    def fwd_pair(t, carry):
        forward(2 * t)
        forward(2 * t + 1)
        return carry

    lax.fori_loop(0, nb // 2, fwd_pair, 0)

    w = w_ref[...]
    part = lax.dot_general(
        jnp.broadcast_to(w, (16, D)), att_ref[...].reshape(T, D), CONTRACT_LAST,
        preferred_element_type=F32)[0:1]
    lmine[...] = part

    def logit_copy(d, slot):
        return pltpu.make_async_remote_copy(
            src_ref=lmine, dst_ref=lrecv.at[slot], send_sem=l_send.at[d], recv_sem=l_recv.at[slot],
            device_id={"head": lax.rem(hd + d, H)}, device_id_type=MESH)

    for d in range(1, H):
        logit_copy(d, hd).start()
    acc[...] = jnp.zeros_like(acc)
    gacc[...] = jnp.zeros_like(gacc)
    logits = part
    for d in range(1, H):
        slot = lax.rem(hd + d, H)
        logit_copy(d, slot).wait_recv()
        logits = logits + lrecv[slot]
    target = lab_ref[...].astype(F32)
    e = jnp.exp(-jnp.abs(logits))
    loss_ref[...] = jnp.maximum(logits, 0.0) + jnp.log1p(e) - target * logits
    sig = jnp.where(logits >= 0, 1.0, e) / (1.0 + e)
    dl = jnp.broadcast_to(sig - target, (8, T)).T[:, 0:1]
    grad_out = up_ref[...].reshape(T, D).astype(F32) + dl * w.astype(F32)
    g_s[...] = grad_out.astype(BF16).reshape(nb, BLOCK, D)

    def backward(i):
        g = g_s[i]
        dp = lax.dot_general(g, gather(vall, i), CONTRACT_LAST, preferred_element_type=F32)
        p = p_s[i]
        rd = jnp.sum(p * dp, axis=-1, keepdims=True)
        ds = (p * (dp - rd) * inv).astype(BF16)
        ds_s[i] = ds
        dk = lax.dot_general(ds, q_ref[i], CONTRACT_FIRST, preferred_element_type=F32)
        dv = lax.dot_general(p.astype(BF16), g, CONTRACT_FIRST, preferred_element_type=F32)
        both = jnp.concatenate([dk, dv], axis=1)
        acc[pl.ds(i, 3)] += both[: 3 * BLOCK].reshape(3, BLOCK, 2 * D)
        rg[pl.ds(i * RAND, RAND)] = (
            both[3 * BLOCK : (3 + RAND) * BLOCK].astype(BF16).reshape(RAND, BLOCK, 2 * D))
        gacc[...] += both[(3 + RAND) * BLOCK :]

    def bwd_pair(t, carry):
        backward(2 * t)
        backward(2 * t + 1)
        return carry

    lax.fori_loop(0, nb // 2, bwd_pair, 0)

    gsend[...] = gacc[...].astype(BF16)
    is_part = lax.rem(me, stride) == 0
    my_part = lax.div(me, jnp.int32(stride))

    def part_copy(j, owner, slot):
        return seq_copy(gsend.at[pl.ds(j * rows, rows)], grecv.at[slot], gp_send.at[j], gp_recv.at[slot], owner)

    for t in range(PARTS):
        j = lax.rem(my_part + t, PARTS)
        owner = j * stride

        @pl.when(owner != me)
        def _():
            part_copy(j, owner, me).start()

    edge_out[0] = acc[0].astype(BF16)
    edge_out[1] = acc[nb + 1].astype(BF16)
    prev, following = lax.rem(me + S - 1, S), lax.rem(me + 1, S)
    to_prev = seq_copy(edge_out.at[0], edge_in.at[1], e_send.at[0], e_recv.at[1], prev)
    to_next = seq_copy(edge_out.at[1], edge_in.at[0], e_send.at[1], e_recv.at[0], following)
    to_prev.start()
    to_next.start()

    order = sorted(range(1, S), key=lambda d: -bin(d // 2).count("1"))

    def out_copy(d, peer, slot):
        return seq_copy(og.at[peer], og_in.at[slot], o_send.at[d], o_recv.at[slot], peer)

    for d in order:
        peer = flip(me, d)
        for t in range(cap):
            og[peer, t] = rg[sidx[peer, t]]
        out_copy(d, peer, me).start()

    def grad_q(i):
        dq_ref[i] = jnp.dot(ds_s[i], gather(kall, i), preferred_element_type=F32)

    def dq_pair(t, carry):
        grad_q(2 * t)
        grad_q(2 * t + 1)
        return carry

    lax.fori_loop(0, nb // 2, dq_pair, 0)

    def take(block, place):
        block = block.astype(F32)
        for b in range(nb):
            acc[1 + b] += block * (place == b).astype(F32)

    for t in range(cap):
        take(rg[sidx[me, t]], roff[me, t])

    def share_copy(d, peer, slot):
        return seq_copy(gsum, gall.at[slot], gb_send.at[d], gb_recv.at[slot], peer)

    @pl.when(is_part)
    def _():
        total = gsend[pl.ds(my_part * rows, rows)].astype(F32)
        for d in range(1, S):
            peer = flip(me, d)
            part_copy(my_part, peer, peer).wait_recv()
            total = total + grecv[peer].astype(F32)
        gsum[...] = total.astype(BF16)
        gall[my_part] = gsum[...]
        for d in range(1, S):
            share_copy(d, flip(me, d), my_part).start()

    for d in sorted(order, key=lambda d: bin(d).count("1")):
        peer = flip(me, d)
        out_copy(d, peer, peer).wait_recv()
        for t in range(cap):
            take(og_in[peer, t], roff[peer, t])

    to_prev.wait_recv()
    to_next.wait_recv()
    acc[1] += edge_in[0].astype(F32)
    acc[nb] += edge_in[1].astype(F32)

    for t in range(PARTS):
        j = lax.rem(my_part + t, PARTS)

        @pl.when(j * stride != me)
        def _():
            share_copy(0, me, j).wait_recv()

    for n in range(GLOBAL):
        count = PARTS // GLOBAL
        block = gall[n * count : (n + 1) * count].astype(F32).reshape(BLOCK, 2 * D)
        take(block, glob_ref[n] - me * nb)

    total = acc[1 : nb + 1]
    dk_ref[...] = total[:, :, :D]
    dv_ref[...] = total[:, :, D:]

    for a, (src, dst) in enumerate(pairs):
        for d in evens + [1]:
            seq_copy(src, dst.at[mine], ag_send.at[a, d], ag_recv.at[a, me], flip(me, d)).wait_send()
        for d in evens:
            part = dst.at[pl.ds(flip(me, d) * nb, nb)]
            seq_copy(part, part, ag_fwd.at[a, d], ag_recv.at[a, me], partner).wait_send()
    for d in range(1, H):
        logit_copy(d, hd).wait_send()
    for t in range(PARTS):
        j = lax.rem(my_part + t, PARTS)
        owner = j * stride

        @pl.when(owner != me)
        def _():
            part_copy(j, owner, me).wait_send()

    to_prev.wait_send()
    to_next.wait_send()
    for d in order:
        peer = flip(me, d)
        out_copy(d, peer, me).wait_send()

    @pl.when(is_part)
    def _():
        for d in range(1, S):
            share_copy(d, flip(me, d), my_part).wait_send()


def body(S, H, queries, key_rows, value_rows, upstream, exit_weight, labels, rand_blocks, glob_blocks):
    T, D = queries.shape
    nb = T // BLOCK
    cap = max(1, (nb * RAND + S - 1) // S)
    W = 2 * D
    rows = GLOBAL * BLOCK // PARTS
    blocked = lambda x: x.reshape(nb, BLOCK, D)
    vmem = pl.BlockSpec(memory_space=pltpu.VMEM)
    smem = pl.BlockSpec(memory_space=pltpu.SMEM)
    dma = pltpu.SemaphoreType.DMA
    att, loss, dq, dk, dv = pl.pallas_call(
        functools.partial(kernel, S, H, nb, D, cap),
        out_shape=(
            jax.ShapeDtypeStruct((nb, BLOCK, D), BF16),
            jax.ShapeDtypeStruct((1, T), F32),
            jax.ShapeDtypeStruct((nb, BLOCK, D), F32),
            jax.ShapeDtypeStruct((nb, BLOCK, D), F32),
            jax.ShapeDtypeStruct((nb, BLOCK, D), F32),
        ),
        in_specs=[vmem] * 6 + [smem] * 2,
        out_specs=[vmem] * 5,
        scratch_shapes=[
            pltpu.VMEM((S * nb, BLOCK, D), BF16),
            pltpu.VMEM((S * nb, BLOCK, D), BF16),
            pltpu.VMEM((nb, BLOCK, SLOTS * BLOCK), F32),
            pltpu.VMEM((nb, BLOCK, SLOTS * BLOCK), BF16),
            pltpu.VMEM((nb, BLOCK, D), BF16),
            pltpu.VMEM((nb * RAND, BLOCK, W), BF16),
            pltpu.VMEM((S, cap, BLOCK, W), BF16),
            pltpu.VMEM((S, cap, BLOCK, W), BF16),
            pltpu.VMEM((nb + 2, BLOCK, W), F32),
            pltpu.VMEM((GLOBAL * BLOCK, W), F32),
            pltpu.VMEM((GLOBAL * BLOCK, W), BF16),
            pltpu.VMEM((S, rows, W), BF16),
            pltpu.VMEM((rows, W), BF16),
            pltpu.VMEM((PARTS, rows, W), BF16),
            pltpu.VMEM((2, BLOCK, W), BF16),
            pltpu.VMEM((2, BLOCK, W), BF16),
            pltpu.VMEM((1, T), F32),
            pltpu.VMEM((H, 1, T), F32),
            pltpu.SMEM((S, cap), jnp.int32),
            pltpu.SMEM((S, cap), jnp.int32),
            dma((2, S)), dma((2, S)), dma((2, S)),
            dma((H,)), dma((H,)),
            dma((S,)), dma((S,)),
            dma((2,)), dma((2,)),
            dma((PARTS,)), dma((S,)),
            dma((S,)), dma((PARTS,)),
        ],
        compiler_params=pltpu.CompilerParams(
            collective_id=0, has_side_effects=True, vmem_limit_bytes=48 * 1024 * 1024),
    )(
        blocked(queries), blocked(key_rows), blocked(value_rows), blocked(upstream),
        exit_weight.reshape(1, D), labels.reshape(1, T), rand_blocks, glob_blocks,
    )
    flat = lambda x: x.reshape(T, D)
    return (flat(att), loss.reshape(T), flat(dq), flat(dk), flat(dv))


def solution(mesh):
    placed = (
        P("seq", "head"),
        P("seq", "head"),
        P("seq", "head"),
        P("seq", "head"),
        P("head"),
        P("seq"),
        P(),
        P(),
    )
    return jax.shard_map(
        functools.partial(body, mesh.shape["seq"], mesh.shape["head"]),
        mesh=mesh,
        in_specs=placed,
        out_specs=(
            P("seq", "head"),
            P("seq"),
            P("seq", "head"),
            P("seq", "head"),
            P("seq", "head"),
        ),
        check_vma=False,
    )
```

```python
import functools
import math

import jax
import jax.numpy as jnp
from jax import lax
from jax.experimental import pallas as pl
from jax.experimental.pallas import tpu as pltpu
from jax.sharding import PartitionSpec as P

BLOCK = 64
RAND = 3
GLOBAL = 2
SLOTS = 3 + RAND + GLOBAL
MESH = pl.DeviceIdType.MESH
F32 = jnp.float32
BF16 = jnp.bfloat16
CONTRACT_LAST = (((1,), (1,)), ((), ()))
CONTRACT_FIRST = (((0,), (0,)), ((), ()))
PARTS = 8
VMEM = 63 * 1024 * 1024


def flip(me, bits):
    out = me
    bit = 1
    while bit <= bits:
        if bits & bit:
            out = out + (1 - 2 * lax.rem(lax.div(me, jnp.int32(bit)), jnp.int32(2))) * bit
        bit *= 2
    return out


def kernel(
    S, H, nb, D, cap,
    q_ref, k_ref, v_ref, up_ref, w_ref, lab_ref, rand_ref, glob_ref,
    att_out, loss_out, dq_out, dk_out, dv_out,
    att_ref, loss_ref, dq_ref, dk_ref, dv_ref, lab_s, q_s, up_s, kall, vall, p_s, pb_s, pt_s, ds_s, dst_s, g_s, og, og_in, acc, gsend, grecv, gsum, gall,
    edge_out, edge_in, lmine, lrecv, sidx, roff,
    in_sem, ag_send, ag_recv, l_send, l_recv, o_send, o_recv, e_send, e_recv,
    gp_send, gp_recv, gb_send, gb_recv, out_sem,
):
    me = lax.axis_index("seq")
    hd = lax.axis_index("head")
    N = S * nb
    inv = 1.0 / math.sqrt(D)
    stride = max(1, S // PARTS)
    rows = GLOBAL * BLOCK // PARTS
    T = nb * BLOCK
    half = nb // 2
    WIN = 3 * BLOCK
    mine = pl.ds(me * nb, nb)

    def seq_copy(src, dst, ssem, rsem, peer):
        return pltpu.make_async_remote_copy(
            src_ref=src, dst_ref=dst, send_sem=ssem, recv_sem=rsem,
            device_id={"seq": peer}, device_id_type=MESH)

    local = [
        pltpu.make_async_copy(src, dst, in_sem.at[n])
        for n, (src, dst) in enumerate(
            ((k_ref, kall.at[mine]), (v_ref, vall.at[mine]), (q_ref, q_s), (up_ref, up_s), (lab_ref, lab_s)))
    ]
    for copy in local:
        copy.start()
    results = [
        pltpu.make_async_copy(src, dst, out_sem.at[n])
        for n, (src, dst) in enumerate(
            ((att_ref, att_out), (loss_ref, loss_out), (dq_ref, dq_out), (dk_ref, dk_out), (dv_ref, dv_out)))
    ]

    barrier = pltpu.get_barrier_semaphore()
    for d in range(1, S):
        pl.semaphore_signal(barrier, inc=1, device_id={"seq": flip(me, d)}, device_id_type=MESH)
    for d in range(1, H):
        pl.semaphore_signal(barrier, inc=1, device_id={"head": lax.rem(hd + d, H)}, device_id_type=MESH)
    pl.semaphore_wait(barrier, S - 1 + H - 1)

    full = ((k_ref, kall), (v_ref, vall))
    partner = flip(me, 1)
    sends = []

    def push(a, n, src, owner, lo, count, piece, peer):
        dst = full[a][1].at[pl.ds(owner * nb + lo, count)]
        copy = seq_copy(dst if src is None else src, dst, ag_send.at[a, n], ag_recv.at[a, owner, piece], peer)
        copy.start()
        sends.append(copy)

    def arrived(a, owner, lo, count, piece):
        part = full[a][1].at[pl.ds(owner * nb + lo, count)]
        seq_copy(part, part, ag_send.at[a, 0], ag_recv.at[a, owner, piece], partner).wait_recv()

    two_step = S == 8
    evens = [2, 4] if two_step else list(range(2, S, 2))

    def own(a):
        for d in evens + [1]:
            push(a, d, full[a][0], me, 0, nb, 0, flip(me, d))

    def relay(a):
        for n, d in enumerate(evens):
            owner = flip(me, d)
            arrived(a, owner, 0, nb, 0)
            if two_step:
                push(a, 8 + n, None, owner, n * half, half, n, flip(me, 6 - d))
            push(a, S + 2 + d, None, owner, 0, nb, 0, partner)

    def corner(a):
        if two_step:
            owner = flip(me, 6)
            for n in range(2):
                arrived(a, owner, n * half, half, n)
                push(a, 5 + 2 * n, None, owner, n * half, half, n, partner)

    def finish(a):
        for d in range(1, S, 2):
            owner = flip(me, d)
            if two_step and d == 7:
                for n in range(2):
                    arrived(a, owner, n * half, half, n)
            else:
                arrived(a, owner, 0, nb, 0)

    own(0)
    own(1)

    def tables(s, carry):
        cnt, cnt2 = jnp.int32(0), jnp.int32(0)
        idx = [jnp.int32(3)] * cap
        off = [jnp.int32(-1)] * cap
        for j in range(nb * RAND):
            b = rand_ref[j % RAND, me * nb + j // RAND]
            hit = lax.div(b, jnp.int32(nb)) == s
            c = rand_ref[j % RAND, s * nb + j // RAND]
            hit2 = lax.div(c, jnp.int32(nb)) == me
            place = lax.rem(c, jnp.int32(nb))
            for t in range(cap):
                idx[t] = jnp.where(hit & (cnt == t), j // RAND * SLOTS + 3 + j % RAND, idx[t])
                off[t] = jnp.where(hit2 & (cnt2 == t), place, off[t])
            cnt = cnt + hit.astype(jnp.int32)
            cnt2 = cnt2 + hit2.astype(jnp.int32)
        for t in range(cap):
            sidx[s, t] = idx[t]
            roff[s, t] = off[t]
        return carry

    lax.fori_loop(0, S, tables, 0)
    acc[...] = jnp.zeros_like(acc)

    relay(0)
    relay(1)
    corner(0)
    finish(0)
    for copy in local:
        copy.wait()

    def gather(all_ref, i):
        gi = me * nb + i
        ids = [lax.rem(gi + N - 1, N), gi, lax.rem(gi + 1, N)]
        ids += [rand_ref[r, gi] for r in range(RAND)]
        ids += [glob_ref[r] for r in range(GLOBAL)]
        return jnp.concatenate([all_ref[b] for b in ids], axis=0)

    def by_slot(x):
        return x.T.astype(BF16).reshape(SLOTS, BLOCK, BLOCK)

    def pairs(lo, hi, step):
        def two(t, carry):
            step(2 * t)
            step(2 * t + 1)
            return carry

        lax.fori_loop(lo, hi, two, 0)

    col = lax.broadcasted_iota(jnp.int32, (BLOCK, SLOTS * BLOCK), 1)

    def softmax(i):
        keys = gather(kall, i)
        s = lax.dot_general(q_s[i], keys, CONTRACT_LAST, preferred_element_type=F32) * inv
        gi = me * nb + i
        low = jnp.where(gi == 0, BLOCK, 0)
        void = (col < low) | ((col >= 2 * BLOCK) & (col < jnp.where(gi == N - 1, 3 * BLOCK, 0)))
        s = jnp.where(void, -jnp.inf, s)
        e = jnp.exp(s - jnp.max(s, axis=-1, keepdims=True))
        p = e * (1.0 / jnp.sum(e, axis=-1, keepdims=True))
        p_s[i] = p
        pb_s[i] = p.astype(BF16)
        pt_s[pl.ds(i * SLOTS, SLOTS)] = by_slot(p)

    pairs(0, nb // 4, softmax)
    corner(1)
    pairs(nb // 4, nb // 2, softmax)
    finish(1)

    def attend(i):
        att_ref[i] = jnp.dot(pb_s[i], gather(vall, i), preferred_element_type=F32).astype(BF16)

    pairs(0, nb // 2, attend)

    w = w_ref[...]
    part = lax.dot_general(
        jnp.broadcast_to(w, (16, D)), att_ref[...].reshape(T, D), CONTRACT_LAST,
        preferred_element_type=F32)[0:1]
    lmine[...] = part

    def logit_copy(d, slot):
        return pltpu.make_async_remote_copy(
            src_ref=lmine, dst_ref=lrecv.at[slot], send_sem=l_send.at[d], recv_sem=l_recv.at[slot],
            device_id={"head": lax.rem(hd + d, H)}, device_id_type=MESH)

    for d in range(1, H):
        logit_copy(d, hd).start()
    results[0].start()
    logits = part
    for d in range(1, H):
        slot = lax.rem(hd + d, H)
        logit_copy(d, slot).wait_recv()
        logits = logits + lrecv[slot]
    target = lab_s[...].astype(F32)
    e = jnp.exp(-jnp.abs(logits))
    loss_ref[...] = jnp.maximum(logits, 0.0) + jnp.log1p(e) - target * logits
    results[1].start()
    sig = jnp.where(logits >= 0, 1.0, e) / (1.0 + e)
    dl = jnp.broadcast_to(sig - target, (8, T)).T[:, 0:1]
    grad_out = up_s[...].reshape(T, D).astype(F32) + dl * w.astype(F32)
    g_s[...] = grad_out.astype(BF16).reshape(nb, BLOCK, D)

    terms = ((dst_s, q_s, ds_s), (pt_s, g_s, pb_s))

    def slot_term(a, e):
        return jnp.dot(terms[a][0][e], terms[a][1][lax.div(e, jnp.int32(SLOTS))], preferred_element_type=F32)

    order = sorted(range(1, S), key=lambda d: (-bin(d // 2).count("1"), d % 2, d))

    def out_copy(a, d, peer, slot):
        return seq_copy(og.at[a, peer], og_in.at[a, slot], o_send.at[a, d], o_recv.at[a, slot], peer)

    def send_random(a):
        for d in order:
            peer = flip(me, d)
            for t in range(cap):
                og[a, peer, t] = slot_term(a, sidx[peer, t]).astype(BF16)
            copy = out_copy(a, d, peer, me)
            copy.start()
            sends.append(copy)

    is_part = lax.rem(me, stride) == 0
    my_part = lax.div(me, jnp.int32(stride))

    def part_copy(a, j, owner, slot):
        return seq_copy(
            gsend.at[a, pl.ds(j * rows, rows)], grecv.at[a, slot], gp_send.at[a, j], gp_recv.at[a, slot], owner)

    def share_copy(a, d, peer, slot):
        return seq_copy(gsum.at[a], gall.at[a, slot], gb_send.at[a, d], gb_recv.at[a, slot], peer)

    def send_global(a):
        both = terms[a][2][:, :, (3 + RAND) * BLOCK :].reshape(T, GLOBAL * BLOCK)
        gsend[a] = lax.dot_general(
            both, terms[a][1][...].reshape(T, D), CONTRACT_FIRST, preferred_element_type=F32).astype(BF16)
        for t in range(PARTS):
            j = lax.rem(my_part + t, PARTS)
            owner = j * stride

            @pl.when(owner != me)
            def _():
                part_copy(a, j, owner, me).start()

    def share_global(a):
        @pl.when(is_part)
        def _():
            total = gsend[a, pl.ds(my_part * rows, rows)].astype(F32)
            for d in range(1, S):
                peer = flip(me, d)
                part_copy(a, my_part, peer, peer).wait_recv()
                total = total + grecv[a, peer].astype(F32)
            gsum[a] = total.astype(BF16)
            gall[a, my_part] = gsum[a]
            for d in range(1, S):
                share_copy(a, d, flip(me, d), my_part).start()

    prev, following = lax.rem(me + S - 1, S), lax.rem(me + 1, S)

    def edge_copies(a):
        return (
            seq_copy(edge_out.at[a, 0], edge_in.at[a, 1], e_send.at[a, 0], e_recv.at[a, 1], prev),
            seq_copy(edge_out.at[a, 1], edge_in.at[a, 0], e_send.at[a, 1], e_recv.at[a, 0], following),
        )

    def window(a):
        def step(i):
            left = terms[a][0][pl.ds(i * SLOTS, 3)].reshape(WIN, BLOCK)
            acc[a, pl.ds(i, 3)] += jnp.dot(
                left, terms[a][1][i], preferred_element_type=F32).reshape(3, BLOCK, D)

        pairs(0, nb // 2, step)
        edge_out[a, 0] = acc[a, 0].astype(BF16)
        edge_out[a, 1] = acc[a, nb + 1].astype(BF16)
        for copy in edge_copies(a):
            copy.start()

    def take(a, blocks, places):
        for b in range(nb):
            value = acc[a, 1 + b]
            for block, place in zip(blocks, places):
                value = value + block * (place == b).astype(F32)
            acc[a, 1 + b] = value

    def take_own(a):
        take(a, [slot_term(a, sidx[me, t]) for t in range(cap)], [roff[me, t] for t in range(cap)])

    def take_random(a):
        for d in sorted(order, key=lambda d: (bin(d).count("1"), d)):
            peer = flip(me, d)
            out_copy(a, d, peer, peer).wait_recv()
            take(a, [og_in[a, peer, t].astype(F32) for t in range(cap)], [roff[peer, t] for t in range(cap)])

    def take_rest(a):
        for copy in edge_copies(a):
            copy.wait_recv()
        acc[a, 1] += edge_in[a, 0].astype(F32)
        acc[a, nb] += edge_in[a, 1].astype(F32)
        for t in range(PARTS):
            j = lax.rem(my_part + t, PARTS)

            @pl.when(j * stride != me)
            def _():
                share_copy(a, 0, me, j).wait_recv()

        count = PARTS // GLOBAL
        blocks = [
            gall[a, n * count : (n + 1) * count].astype(F32).reshape(BLOCK, D) for n in range(GLOBAL)]
        take(a, blocks, [glob_ref[n] - me * nb for n in range(GLOBAL)])

    send_global(1)
    send_random(1)

    def score_grad(i):
        dp = lax.dot_general(g_s[i], gather(vall, i), CONTRACT_LAST, preferred_element_type=F32)
        p = p_s[i]
        rd = jnp.sum(p * dp, axis=-1, keepdims=True)
        ds = p * (dp - rd) * inv
        ds_s[i] = ds.astype(BF16)
        dst_s[pl.ds(i * SLOTS, SLOTS)] = by_slot(ds)

    pairs(0, nb // 2, score_grad)
    share_global(1)
    send_global(0)
    send_random(0)
    window(0)
    window(1)
    share_global(0)

    def grad_q(i):
        dq_ref[i] = jnp.dot(ds_s[i], gather(kall, i), preferred_element_type=F32)

    pairs(0, nb // 2, grad_q)
    results[2].start()
    take_own(1)
    take_own(0)
    take_random(1)
    take_rest(1)
    dv_ref[...] = acc[1, 1 : nb + 1]
    results[4].start()
    take_random(0)
    take_rest(0)
    dk_ref[...] = acc[0, 1 : nb + 1]
    results[3].start()

    for copy in results:
        copy.wait()
    for copy in sends:
        copy.wait_send()
    for d in range(1, H):
        logit_copy(d, hd).wait_send()
    for a in range(2):
        for t in range(PARTS):
            j = lax.rem(my_part + t, PARTS)
            owner = j * stride

            @pl.when(owner != me)
            def _():
                part_copy(a, j, owner, me).wait_send()

        for copy in edge_copies(a):
            copy.wait_send()

        @pl.when(is_part)
        def _():
            for d in range(1, S):
                share_copy(a, d, flip(me, d), my_part).wait_send()


def store(*refs):
    count = len(refs) // 2
    copies = [
        pltpu.make_async_copy(refs[n], refs[count + n], refs[-1].at[n]) for n in range(count)]
    for copy in copies:
        copy.start()
    for copy in copies:
        copy.wait()


def body(S, H, queries, key_rows, value_rows, upstream, exit_weight, labels, rand_blocks, glob_blocks):
    T, D = queries.shape
    nb = T // BLOCK
    cap = max(1, (nb * RAND + S - 1) // S)
    rows = GLOBAL * BLOCK // PARTS
    blocked = lambda x: x.reshape(nb, BLOCK, D)
    vmem = pl.BlockSpec(memory_space=pltpu.VMEM)
    smem = pl.BlockSpec(memory_space=pltpu.SMEM)
    hbm = pl.BlockSpec(memory_space=pltpu.HBM)
    dma = pltpu.SemaphoreType.DMA
    results = (
        jax.ShapeDtypeStruct((nb, BLOCK, D), BF16),
        jax.ShapeDtypeStruct((1, T), F32),
        jax.ShapeDtypeStruct((nb, BLOCK, D), F32),
        jax.ShapeDtypeStruct((nb, BLOCK, D), F32),
        jax.ShapeDtypeStruct((nb, BLOCK, D), F32),
    )
    done = pl.pallas_call(
        functools.partial(kernel, S, H, nb, D, cap),
        out_shape=results,
        in_specs=[hbm] * 4 + [vmem, hbm] + [smem] * 2,
        out_specs=[hbm] * 5,
        scratch_shapes=[pltpu.VMEM(x.shape, x.dtype) for x in results] + [
            pltpu.VMEM((1, T), jnp.int32),
            pltpu.VMEM((nb, BLOCK, D), BF16),
            pltpu.VMEM((nb, BLOCK, D), BF16),
            pltpu.VMEM((S * nb, BLOCK, D), BF16),
            pltpu.VMEM((S * nb, BLOCK, D), BF16),
            pltpu.VMEM((nb, BLOCK, SLOTS * BLOCK), F32),
            pltpu.VMEM((nb, BLOCK, SLOTS * BLOCK), BF16),
            pltpu.VMEM((nb * SLOTS, BLOCK, BLOCK), BF16),
            pltpu.VMEM((nb, BLOCK, SLOTS * BLOCK), BF16),
            pltpu.VMEM((nb * SLOTS, BLOCK, BLOCK), BF16),
            pltpu.VMEM((nb, BLOCK, D), BF16),
            pltpu.VMEM((2, S, cap, BLOCK, D), BF16),
            pltpu.VMEM((2, S, cap, BLOCK, D), BF16),
            pltpu.VMEM((2, nb + 2, BLOCK, D), F32),
            pltpu.VMEM((2, GLOBAL * BLOCK, D), BF16),
            pltpu.VMEM((2, S, rows, D), BF16),
            pltpu.VMEM((2, rows, D), BF16),
            pltpu.VMEM((2, PARTS, rows, D), BF16),
            pltpu.VMEM((2, 2, BLOCK, D), BF16),
            pltpu.VMEM((2, 2, BLOCK, D), BF16),
            pltpu.VMEM((1, T), F32),
            pltpu.VMEM((H, 1, T), F32),
            pltpu.SMEM((S, cap), jnp.int32),
            pltpu.SMEM((S, cap), jnp.int32),
            dma((5,)),
            dma((2, 2 * S + 2)), dma((2, S, 2)),
            dma((H,)), dma((H,)),
            dma((2, S)), dma((2, S)),
            dma((2, 2)), dma((2, 2)),
            dma((2, PARTS)), dma((2, S)),
            dma((2, S)), dma((2, PARTS)), dma((5,)),
        ],
        compiler_params=pltpu.CompilerParams(
            collective_id=0, has_side_effects=True, vmem_limit_bytes=VMEM),
    )(
        blocked(queries), blocked(key_rows), blocked(value_rows), blocked(upstream),
        exit_weight.reshape(1, D), labels.reshape(1, T), rand_blocks.T, glob_blocks,
    )
    att, loss, dq, dk, dv = pl.pallas_call(
        store,
        out_shape=results,
        in_specs=[hbm] * 5,
        out_specs=[hbm] * 5,
        scratch_shapes=[dma((5,))],
        compiler_params=pltpu.CompilerParams(vmem_limit_bytes=VMEM),
    )(*done)
    flat = lambda x: x.reshape(T, D)
    return (flat(att), loss.reshape(T), flat(dq), flat(dk), flat(dv))


def solution(mesh):
    placed = (
        P("seq", "head"),
        P("seq", "head"),
        P("seq", "head"),
        P("seq", "head"),
        P("head"),
        P("seq"),
        P(),
        P(),
    )
    return jax.shard_map(
        functools.partial(body, mesh.shape["seq"], mesh.shape["head"]),
        mesh=mesh,
        in_specs=placed,
        out_specs=(
            P("seq", "head"),
            P("seq"),
            P("seq", "head"),
            P("seq", "head"),
            P("seq", "head"),
        ),
        check_vma=False,
    )
```

```python
import functools
import math

import jax
import jax.numpy as jnp
from jax import lax
from jax.experimental import pallas as pl
from jax.experimental.pallas import tpu as pltpu
from jax.sharding import PartitionSpec as P

BLOCK = 64
RAND = 3
GLOBAL = 2
SLOTS = 3 + RAND + GLOBAL
MESH = pl.DeviceIdType.MESH
F32 = jnp.float32
BF16 = jnp.bfloat16
CONTRACT_LAST = (((1,), (1,)), ((), ()))
CONTRACT_FIRST = (((0,), (0,)), ((), ()))
PARTS = 8
VMEM = 63 * 1024 * 1024


def flip(me, bits):
    out = me
    bit = 1
    while bit <= bits:
        if bits & bit:
            out = out + (1 - 2 * lax.rem(lax.div(me, jnp.int32(bit)), jnp.int32(2))) * bit
        bit *= 2
    return out


def kernel(
    S, H, nb, D, cap,
    q_ref, k_ref, v_ref, up_ref, w_ref, lab_ref, rand_ref, glob_ref,
    att_out, loss_out, dq_out, dk_out, dv_out,
    att_ref, loss_ref, dq_ref, dk_ref, dv_ref, lab_s, q_s, up_s, kall, vall, p_s, pb_s, pt_s, ds_s, dst_s, g_s, og, og_in, acc, gsend, grecv, gsum, gall,
    edge_out, edge_in, lmine, lrecv, sidx, roff,
    in_sem, ag_send, ag_recv, l_send, l_recv, o_send, o_recv, e_send, e_recv,
    gp_send, gp_recv, gb_send, gb_recv, out_sem,
):
    me = lax.axis_index("seq")
    hd = lax.axis_index("head")
    N = S * nb
    inv = 1.0 / math.sqrt(D)
    stride = max(1, S // PARTS)
    rows = GLOBAL * BLOCK // PARTS
    T = nb * BLOCK
    half = nb // 2
    WIN = 3 * BLOCK
    mine = pl.ds(me * nb, nb)

    def seq_copy(src, dst, ssem, rsem, peer):
        return pltpu.make_async_remote_copy(
            src_ref=src, dst_ref=dst, send_sem=ssem, recv_sem=rsem,
            device_id={"seq": peer}, device_id_type=MESH)

    local = [
        pltpu.make_async_copy(src, dst, in_sem.at[n])
        for n, (src, dst) in enumerate(
            ((k_ref, kall.at[mine]), (v_ref, vall.at[mine]), (q_ref, q_s), (up_ref, up_s), (lab_ref, lab_s)))
    ]
    for copy in local:
        copy.start()
    results = [
        pltpu.make_async_copy(src, dst, out_sem.at[n])
        for n, (src, dst) in enumerate(
            ((att_ref, att_out), (loss_ref, loss_out), (dq_ref, dq_out), (dk_ref, dk_out), (dv_ref, dv_out)))
    ]

    barrier = pltpu.get_barrier_semaphore()
    for d in range(1, S):
        pl.semaphore_signal(barrier, inc=1, device_id={"seq": flip(me, d)}, device_id_type=MESH)
    for d in range(1, H):
        pl.semaphore_signal(barrier, inc=1, device_id={"head": lax.rem(hd + d, H)}, device_id_type=MESH)
    pl.semaphore_wait(barrier, S - 1 + H - 1)

    full = (kall, vall)
    partner = flip(me, 1)
    sends = []

    def push(a, n, owner, lo, count, piece, peer):
        part = full[a].at[pl.ds(owner * nb + lo, count)]
        copy = seq_copy(part, part, ag_send.at[a, n], ag_recv.at[a, owner, piece], peer)
        copy.start()
        sends.append(copy)

    def arrived(a, owner, lo, count, piece):
        part = full[a].at[pl.ds(owner * nb + lo, count)]
        seq_copy(part, part, ag_send.at[a, 0], ag_recv.at[a, owner, piece], partner).wait_recv()

    two_step = S == 8
    evens = [2, 4] if two_step else list(range(2, S, 2))

    def own(a):
        for d in evens + [1]:
            push(a, d, me, 0, nb, 0, flip(me, d))

    def relay(a):
        for n, d in enumerate(evens):
            owner = flip(me, d)
            arrived(a, owner, 0, nb, 0)
            if two_step:
                push(a, 8 + n, owner, n * half, half, n, flip(me, 6 - d))
            push(a, S + 2 + d, owner, 0, nb, 0, partner)

    def corner(a):
        if two_step:
            owner = flip(me, 6)
            for n in range(2):
                arrived(a, owner, n * half, half, n)
                push(a, 5 + 2 * n, owner, n * half, half, n, partner)

    def finish(a):
        for d in range(1, S, 2):
            owner = flip(me, d)
            if two_step and d == 7:
                for n in range(2):
                    arrived(a, owner, n * half, half, n)
            else:
                arrived(a, owner, 0, nb, 0)

    for a in range(2):
        local[a].wait()
        own(a)

    def tables(s, carry):
        cnt, cnt2 = jnp.int32(0), jnp.int32(0)
        idx = [jnp.int32(3)] * cap
        off = [jnp.int32(-1)] * cap
        for j in range(nb * RAND):
            b = rand_ref[j % RAND, me * nb + j // RAND] - s * nb
            hit = (b >= 0) & (b < nb)
            place = rand_ref[j % RAND, s * nb + j // RAND] - me * nb
            hit2 = (place >= 0) & (place < nb)
            for t in range(cap):
                idx[t] = jnp.where(hit & (cnt == t), j // RAND * SLOTS + 3 + j % RAND, idx[t])
                off[t] = jnp.where(hit2 & (cnt2 == t), place, off[t])
            cnt = cnt + hit.astype(jnp.int32)
            cnt2 = cnt2 + hit2.astype(jnp.int32)
        for t in range(cap):
            sidx[s, t] = idx[t]
            roff[s, t] = off[t]
        return carry

    lax.fori_loop(0, S, tables, 0)
    acc[...] = jnp.zeros_like(acc)

    relay(0)
    relay(1)
    corner(0)
    finish(0)
    for copy in local[2:]:
        copy.wait()

    def gather(all_ref, i):
        gi = me * nb + i
        ids = [lax.rem(gi + N - 1, N), gi, lax.rem(gi + 1, N)]
        ids += [rand_ref[r, gi] for r in range(RAND)]
        ids += [glob_ref[r] for r in range(GLOBAL)]
        return jnp.concatenate([all_ref[b] for b in ids], axis=0)

    def by_slot(x):
        return x.T.astype(BF16).reshape(SLOTS, BLOCK, BLOCK)

    def pairs(lo, hi, step):
        def two(t, carry):
            step(2 * t)
            step(2 * t + 1)
            return carry

        lax.fori_loop(lo, hi, two, 0)

    col = lax.broadcasted_iota(jnp.int32, (BLOCK, SLOTS * BLOCK), 1)

    def softmax(i):
        keys = gather(kall, i)
        s = lax.dot_general(q_s[i], keys, CONTRACT_LAST, preferred_element_type=F32) * inv
        gi = me * nb + i
        low = jnp.where(gi == 0, BLOCK, 0)
        void = (col < low) | ((col >= 2 * BLOCK) & (col < jnp.where(gi == N - 1, 3 * BLOCK, 0)))
        s = jnp.where(void, -jnp.inf, s)
        e = jnp.exp(s - jnp.max(s, axis=-1, keepdims=True))
        p = e * (1.0 / jnp.sum(e, axis=-1, keepdims=True))
        p_s[i] = p
        pb_s[i] = p.astype(BF16)
        pt_s[pl.ds(i * SLOTS, SLOTS)] = by_slot(p)

    pairs(0, nb // 4, softmax)
    corner(1)
    pairs(nb // 4, nb // 2, softmax)
    finish(1)

    def attend(i):
        att_ref[i] = jnp.dot(pb_s[i], gather(vall, i), preferred_element_type=F32).astype(BF16)

    pairs(0, nb // 2, attend)

    w = w_ref[...]
    part = lax.dot_general(
        jnp.broadcast_to(w, (16, D)), att_ref[...].reshape(T, D), CONTRACT_LAST,
        preferred_element_type=F32)[0:1]
    lmine[...] = part

    def logit_copy(d, slot):
        return pltpu.make_async_remote_copy(
            src_ref=lmine, dst_ref=lrecv.at[slot], send_sem=l_send.at[d], recv_sem=l_recv.at[slot],
            device_id={"head": lax.rem(hd + d, H)}, device_id_type=MESH)

    for d in range(1, H):
        logit_copy(d, hd).start()
    results[0].start()
    logits = part
    for d in range(1, H):
        slot = lax.rem(hd + d, H)
        logit_copy(d, slot).wait_recv()
        logits = logits + lrecv[slot]
    target = lab_s[...].astype(F32)
    e = jnp.exp(-jnp.abs(logits))
    loss_ref[...] = jnp.maximum(logits, 0.0) + jnp.log1p(e) - target * logits
    results[1].start()
    sig = jnp.where(logits >= 0, 1.0, e) / (1.0 + e)
    dl = jnp.broadcast_to(sig - target, (8, T)).T[:, 0:1]
    grad_out = up_s[...].reshape(T, D).astype(F32) + dl * w.astype(F32)
    g_s[...] = grad_out.astype(BF16).reshape(nb, BLOCK, D)

    terms = ((dst_s, q_s, ds_s), (pt_s, g_s, pb_s))

    def slot_term(a, e):
        return jnp.dot(terms[a][0][e], terms[a][1][lax.div(e, jnp.int32(SLOTS))], preferred_element_type=F32)

    order = sorted(range(1, S), key=lambda d: (-bin(d // 2).count("1"), d % 2, d))

    def out_copy(a, d, peer, slot):
        return seq_copy(og.at[a, peer], og_in.at[a, slot], o_send.at[a, d], o_recv.at[a, slot], peer)

    def send_random(a):
        for d in order:
            peer = flip(me, d)
            for t in range(cap):
                og[a, peer, t] = slot_term(a, sidx[peer, t]).astype(BF16)
            copy = out_copy(a, d, peer, me)
            copy.start()
            sends.append(copy)

    is_part = lax.rem(me, stride) == 0
    my_part = lax.div(me, jnp.int32(stride))

    def part_copy(a, j, owner, slot):
        return seq_copy(
            gsend.at[a, pl.ds(j * rows, rows)], grecv.at[a, slot], gp_send.at[a, j], gp_recv.at[a, slot], owner)

    def share_copy(a, d, peer, slot):
        return seq_copy(gsum.at[a], gall.at[a, slot], gb_send.at[a, d], gb_recv.at[a, slot], peer)

    def send_global(a):
        both = terms[a][2][:, :, (3 + RAND) * BLOCK :].reshape(T, GLOBAL * BLOCK)
        gsend[a] = lax.dot_general(
            both, terms[a][1][...].reshape(T, D), CONTRACT_FIRST, preferred_element_type=F32).astype(BF16)
        for t in range(PARTS):
            j = lax.rem(my_part + t, PARTS)
            owner = j * stride

            @pl.when(owner != me)
            def _():
                part_copy(a, j, owner, me).start()

    def share_global(a):
        @pl.when(is_part)
        def _():
            total = gsend[a, pl.ds(my_part * rows, rows)].astype(F32)
            for d in range(1, S):
                peer = flip(me, d)
                part_copy(a, my_part, peer, peer).wait_recv()
                total = total + grecv[a, peer].astype(F32)
            gsum[a] = total.astype(BF16)
            gall[a, my_part] = gsum[a]
            for d in range(1, S):
                share_copy(a, d, flip(me, d), my_part).start()

    prev, following = lax.rem(me + S - 1, S), lax.rem(me + 1, S)

    def edge_copies(a):
        return (
            seq_copy(edge_out.at[a, 0], edge_in.at[a, 1], e_send.at[a, 0], e_recv.at[a, 1], prev),
            seq_copy(edge_out.at[a, 1], edge_in.at[a, 0], e_send.at[a, 1], e_recv.at[a, 0], following),
        )

    def window(a):
        def step(i):
            left = terms[a][0][pl.ds(i * SLOTS, 3)].reshape(WIN, BLOCK)
            acc[a, pl.ds(i, 3)] += jnp.dot(
                left, terms[a][1][i], preferred_element_type=F32).reshape(3, BLOCK, D)

        pairs(0, nb // 2, step)
        edge_out[a, 0] = acc[a, 0].astype(BF16)
        edge_out[a, 1] = acc[a, nb + 1].astype(BF16)
        for copy in edge_copies(a):
            copy.start()

    def take(a, blocks, places):
        for b in range(nb):
            value = acc[a, 1 + b]
            for block, place in zip(blocks, places):
                value = value + block * (place == b).astype(F32)
            acc[a, 1 + b] = value

    def take_own(a):
        take(a, [slot_term(a, sidx[me, t]) for t in range(cap)], [roff[me, t] for t in range(cap)])

    def take_random(a):
        for d in sorted(order, key=lambda d: (bin(d).count("1"), d)):
            peer = flip(me, d)
            out_copy(a, d, peer, peer).wait_recv()
            take(a, [og_in[a, peer, t].astype(F32) for t in range(cap)], [roff[peer, t] for t in range(cap)])

    def take_rest(a):
        for copy in edge_copies(a):
            copy.wait_recv()
        acc[a, 1] += edge_in[a, 0].astype(F32)
        acc[a, nb] += edge_in[a, 1].astype(F32)
        for t in range(PARTS):
            j = lax.rem(my_part + t, PARTS)

            @pl.when(j * stride != me)
            def _():
                share_copy(a, 0, me, j).wait_recv()

        count = PARTS // GLOBAL
        blocks = [
            gall[a, n * count : (n + 1) * count].astype(F32).reshape(BLOCK, D) for n in range(GLOBAL)]
        take(a, blocks, [glob_ref[n] - me * nb for n in range(GLOBAL)])

    send_global(1)
    send_random(1)

    def score_grad(i):
        dp = lax.dot_general(g_s[i], gather(vall, i), CONTRACT_LAST, preferred_element_type=F32)
        p = p_s[i]
        rd = jnp.sum(p * dp, axis=-1, keepdims=True)
        ds = p * (dp - rd) * inv
        ds_s[i] = ds.astype(BF16)
        dst_s[pl.ds(i * SLOTS, SLOTS)] = by_slot(ds)

    pairs(0, nb // 2, score_grad)
    share_global(1)
    send_global(0)
    send_random(0)
    window(0)
    window(1)
    share_global(0)

    def grad_q(i):
        dq_ref[i] = jnp.dot(ds_s[i], gather(kall, i), preferred_element_type=F32)

    pairs(0, nb // 2, grad_q)
    results[2].start()
    take_own(1)
    take_own(0)
    take_random(1)
    take_rest(1)
    dv_ref[...] = acc[1, 1 : nb + 1]
    results[4].start()
    take_random(0)
    take_rest(0)
    dk_ref[...] = acc[0, 1 : nb + 1]
    results[3].start()

    for copy in results:
        copy.wait()
    for copy in sends:
        copy.wait_send()
    for d in range(1, H):
        logit_copy(d, hd).wait_send()
    for a in range(2):
        for t in range(PARTS):
            j = lax.rem(my_part + t, PARTS)
            owner = j * stride

            @pl.when(owner != me)
            def _():
                part_copy(a, j, owner, me).wait_send()

        for copy in edge_copies(a):
            copy.wait_send()

        @pl.when(is_part)
        def _():
            for d in range(1, S):
                share_copy(a, d, flip(me, d), my_part).wait_send()


def store(*refs):
    count = (len(refs) - 2) // 3
    src, dst, buf = (refs[n * count : (n + 1) * count] for n in range(3))
    loads = [pltpu.make_async_copy(src[n], buf[n], refs[-2].at[n]) for n in range(count)]
    stores = [pltpu.make_async_copy(buf[n], dst[n], refs[-1].at[n]) for n in range(count)]
    for copy in loads:
        copy.start()
    for load, copy in zip(loads, stores):
        load.wait()
        copy.start()
    for copy in stores:
        copy.wait()


def body(S, H, queries, key_rows, value_rows, upstream, exit_weight, labels, rand_blocks, glob_blocks):
    T, D = queries.shape
    nb = T // BLOCK
    cap = max(1, (nb * RAND + S - 1) // S)
    rows = GLOBAL * BLOCK // PARTS
    blocked = lambda x: x.reshape(nb, BLOCK, D)
    vmem = pl.BlockSpec(memory_space=pltpu.VMEM)
    smem = pl.BlockSpec(memory_space=pltpu.SMEM)
    hbm = pl.BlockSpec(memory_space=pltpu.HBM)
    dma = pltpu.SemaphoreType.DMA
    results = (
        jax.ShapeDtypeStruct((nb, BLOCK, D), BF16),
        jax.ShapeDtypeStruct((1, T), F32),
        jax.ShapeDtypeStruct((nb, BLOCK, D), F32),
        jax.ShapeDtypeStruct((nb, BLOCK, D), F32),
        jax.ShapeDtypeStruct((nb, BLOCK, D), F32),
    )
    done = pl.pallas_call(
        functools.partial(kernel, S, H, nb, D, cap),
        out_shape=results,
        in_specs=[hbm] * 4 + [vmem, hbm] + [smem] * 2,
        out_specs=[hbm] * 5,
        scratch_shapes=[pltpu.VMEM(x.shape, x.dtype) for x in results] + [
            pltpu.VMEM((1, T), jnp.int32),
            pltpu.VMEM((nb, BLOCK, D), BF16),
            pltpu.VMEM((nb, BLOCK, D), BF16),
            pltpu.VMEM((S * nb, BLOCK, D), BF16),
            pltpu.VMEM((S * nb, BLOCK, D), BF16),
            pltpu.VMEM((nb, BLOCK, SLOTS * BLOCK), F32),
            pltpu.VMEM((nb, BLOCK, SLOTS * BLOCK), BF16),
            pltpu.VMEM((nb * SLOTS, BLOCK, BLOCK), BF16),
            pltpu.VMEM((nb, BLOCK, SLOTS * BLOCK), BF16),
            pltpu.VMEM((nb * SLOTS, BLOCK, BLOCK), BF16),
            pltpu.VMEM((nb, BLOCK, D), BF16),
            pltpu.VMEM((2, S, cap, BLOCK, D), BF16),
            pltpu.VMEM((2, S, cap, BLOCK, D), BF16),
            pltpu.VMEM((2, nb + 2, BLOCK, D), F32),
            pltpu.VMEM((2, GLOBAL * BLOCK, D), BF16),
            pltpu.VMEM((2, S, rows, D), BF16),
            pltpu.VMEM((2, rows, D), BF16),
            pltpu.VMEM((2, PARTS, rows, D), BF16),
            pltpu.VMEM((2, 2, BLOCK, D), BF16),
            pltpu.VMEM((2, 2, BLOCK, D), BF16),
            pltpu.VMEM((1, T), F32),
            pltpu.VMEM((H, 1, T), F32),
            pltpu.SMEM((S, cap), jnp.int32),
            pltpu.SMEM((S, cap), jnp.int32),
            dma((5,)),
            dma((2, 2 * S + 2)), dma((2, S, 2)),
            dma((H,)), dma((H,)),
            dma((2, S)), dma((2, S)),
            dma((2, 2)), dma((2, 2)),
            dma((2, PARTS)), dma((2, S)),
            dma((2, S)), dma((2, PARTS)), dma((5,)),
        ],
        compiler_params=pltpu.CompilerParams(
            collective_id=0, has_side_effects=True, vmem_limit_bytes=VMEM),
    )(
        blocked(queries), blocked(key_rows), blocked(value_rows), blocked(upstream),
        exit_weight.reshape(1, D), labels.reshape(1, T), rand_blocks.T, glob_blocks,
    )
    att, loss, dq, dk, dv = pl.pallas_call(
        store,
        out_shape=results,
        in_specs=[hbm] * 5,
        out_specs=[hbm] * 5,
        scratch_shapes=[pltpu.VMEM(x.shape, x.dtype) for x in results] + [dma((5,))] * 2,
        compiler_params=pltpu.CompilerParams(vmem_limit_bytes=VMEM),
    )(*done)
    flat = lambda x: x.reshape(T, D)
    return (flat(att), loss.reshape(T), flat(dq), flat(dk), flat(dv))


def solution(mesh):
    placed = (
        P("seq", "head"),
        P("seq", "head"),
        P("seq", "head"),
        P("seq", "head"),
        P("head"),
        P("seq"),
        P(),
        P(),
    )
    return jax.shard_map(
        functools.partial(body, mesh.shape["seq"], mesh.shape["head"]),
        mesh=mesh,
        in_specs=placed,
        out_specs=(
            P("seq", "head"),
            P("seq"),
            P("seq", "head"),
            P("seq", "head"),
            P("seq", "head"),
        ),
        check_vma=False,
    )
```

```python
import functools
import math

import jax
import jax.numpy as jnp
from jax import lax
from jax.experimental import pallas as pl
from jax.experimental.pallas import tpu as pltpu
from jax.sharding import PartitionSpec as P

BLOCK = 64
RAND = 3
GLOBAL = 2
SLOTS = 3 + RAND + GLOBAL
MESH = pl.DeviceIdType.MESH
F32 = jnp.float32
BF16 = jnp.bfloat16
CONTRACT_LAST = (((1,), (1,)), ((), ()))
CONTRACT_FIRST = (((0,), (0,)), ((), ()))
PARTS = 8
VMEM = 63 * 1024 * 1024


def flip(me, bits):
    out = me
    bit = 1
    while bit <= bits:
        if bits & bit:
            out = out + (1 - 2 * lax.rem(lax.div(me, jnp.int32(bit)), jnp.int32(2))) * bit
        bit *= 2
    return out


def xor(x, y, n):
    out = jnp.int32(0)
    bit = 1
    while bit < n:
        a = lax.rem(lax.div(x, jnp.int32(bit)), jnp.int32(2))
        b = lax.rem(lax.div(y, jnp.int32(bit)), jnp.int32(2))
        out = out + (a + b - 2 * a * b) * bit
        bit *= 2
    return out


def kernel(
    S, H, nb, D, cap,
    q_ref, k_ref, v_ref, up_ref, w_ref, lab_ref, rand_ref, glob_ref,
    att_out, loss_out, dq_out, dk_out, dv_out,
    att_ref, loss_ref, dq_ref, dk_ref, dv_ref, lab_s, q_s, up_s, kall, vall, p_s, pb_s, pt_s, ds_s, dst_s, g_s, og, og_in, acc, gsend, grecv, gsum, gall,
    edge_out, edge_in, lmine, lrecv, sidx, roff,
    in_sem, ag_send, ag_recv, l_send, l_recv, o_send, o_recv, e_send, e_recv,
    gp_send, gp_recv, gb_send, gb_recv, out_sem,
):
    me = lax.axis_index("seq")
    hd = lax.axis_index("head")
    N = S * nb
    inv = 1.0 / math.sqrt(D)
    stride = max(1, S // PARTS)
    rows = GLOBAL * BLOCK // PARTS
    T = nb * BLOCK
    half = nb // 2
    WIN = 3 * BLOCK
    mine = pl.ds(me * nb, nb)

    def seq_copy(src, dst, ssem, rsem, peer):
        return pltpu.make_async_remote_copy(
            src_ref=src, dst_ref=dst, send_sem=ssem, recv_sem=rsem,
            device_id={"seq": peer}, device_id_type=MESH)

    local = [
        pltpu.make_async_copy(src, dst, in_sem.at[n])
        for n, (src, dst) in enumerate(
            ((k_ref, kall.at[mine]), (v_ref, vall.at[mine]), (q_ref, q_s), (up_ref, up_s), (lab_ref, lab_s)))
    ]
    for copy in local:
        copy.start()
    results = [
        pltpu.make_async_copy(src, dst, out_sem.at[n])
        for n, (src, dst) in enumerate(
            ((att_ref, att_out), (loss_ref, loss_out), (dq_ref, dq_out), (dk_ref, dk_out), (dv_ref, dv_out)))
    ]

    barrier = pltpu.get_barrier_semaphore()
    for d in range(1, S):
        pl.semaphore_signal(barrier, inc=1, device_id={"seq": flip(me, d)}, device_id_type=MESH)
    for d in range(1, H):
        pl.semaphore_signal(barrier, inc=1, device_id={"head": lax.rem(hd + d, H)}, device_id_type=MESH)
    pl.semaphore_wait(barrier, S - 1 + H - 1)

    full = (kall, vall)
    partner = flip(me, 1)
    sends = []

    def push(a, n, owner, lo, count, piece, peer):
        part = full[a].at[pl.ds(owner * nb + lo, count)]
        copy = seq_copy(part, part, ag_send.at[a, n], ag_recv.at[a, owner, piece], peer)
        copy.start()
        sends.append(copy)

    def arrived(a, owner, lo, count, piece):
        part = full[a].at[pl.ds(owner * nb + lo, count)]
        seq_copy(part, part, ag_send.at[a, 0], ag_recv.at[a, owner, piece], partner).wait_recv()

    two_step = S == 8
    evens = [2, 4] if two_step else list(range(2, S, 2))

    def own(a):
        for d in evens + [1]:
            push(a, d, me, 0, nb, 0, flip(me, d))

    def relay(a):
        for n, d in enumerate(evens):
            owner = flip(me, d)
            arrived(a, owner, 0, nb, 0)
            if two_step:
                push(a, 8 + n, owner, n * half, half, n, flip(me, 6 - d))
            push(a, S + 2 + d, owner, 0, nb, 0, partner)

    def corner(a):
        if two_step:
            owner = flip(me, 6)
            for n in range(2):
                arrived(a, owner, n * half, half, n)
                push(a, 5 + 2 * n, owner, n * half, half, n, partner)

    def finish(a):
        for d in range(1, S, 2):
            owner = flip(me, d)
            if two_step and d == 7:
                for n in range(2):
                    arrived(a, owner, n * half, half, n)
            else:
                arrived(a, owner, 0, nb, 0)

    for a in range(2):
        local[a].wait()
        own(a)

    def tables(s, carry):
        cnt, cnt2 = jnp.int32(0), jnp.int32(0)
        idx = [jnp.int32(3)] * cap
        off = [jnp.int32(-1)] * cap
        for j in range(nb * RAND):
            b = rand_ref[j % RAND, me * nb + j // RAND] - s * nb
            hit = (b >= 0) & (b < nb)
            place = rand_ref[j % RAND, s * nb + j // RAND] - me * nb
            hit2 = (place >= 0) & (place < nb)
            for t in range(cap):
                idx[t] = jnp.where(hit & (cnt == t), j // RAND * SLOTS + 3 + j % RAND, idx[t])
                off[t] = jnp.where(hit2 & (cnt2 == t), place, off[t])
            cnt = cnt + hit.astype(jnp.int32)
            cnt2 = cnt2 + hit2.astype(jnp.int32)
        for t in range(cap):
            sidx[s, t] = idx[t]
            roff[s, t] = off[t]
        return carry

    lax.fori_loop(0, S, tables, 0)
    acc[...] = jnp.zeros_like(acc)

    relay(0)
    relay(1)
    corner(0)
    finish(0)
    for copy in local[2:]:
        copy.wait()

    def gather(all_ref, i):
        gi = me * nb + i
        ids = [lax.rem(gi + N - 1, N), gi, lax.rem(gi + 1, N)]
        ids += [rand_ref[r, gi] for r in range(RAND)]
        ids += [glob_ref[r] for r in range(GLOBAL)]
        return jnp.concatenate([all_ref[b] for b in ids], axis=0)

    def by_slot(x):
        return x.T.astype(BF16).reshape(SLOTS, BLOCK, BLOCK)

    def pairs(lo, hi, step):
        def two(t, carry):
            step(2 * t)
            step(2 * t + 1)
            return carry

        lax.fori_loop(lo, hi, two, 0)

    col = lax.broadcasted_iota(jnp.int32, (BLOCK, SLOTS * BLOCK), 1)

    def softmax(i):
        keys = gather(kall, i)
        s = lax.dot_general(q_s[i], keys, CONTRACT_LAST, preferred_element_type=F32) * inv
        gi = me * nb + i
        low = jnp.where(gi == 0, BLOCK, 0)
        void = (col < low) | ((col >= 2 * BLOCK) & (col < jnp.where(gi == N - 1, 3 * BLOCK, 0)))
        s = jnp.where(void, -jnp.inf, s)
        e = jnp.exp(s - jnp.max(s, axis=-1, keepdims=True))
        p = e * (1.0 / jnp.sum(e, axis=-1, keepdims=True))
        p_s[i] = p
        pb_s[i] = p.astype(BF16)
        pt_s[pl.ds(i * SLOTS, SLOTS)] = by_slot(p)

    pairs(0, nb // 4, softmax)
    corner(1)
    pairs(nb // 4, nb // 2, softmax)
    finish(1)

    def attend(i):
        att_ref[i] = jnp.dot(pb_s[i], gather(vall, i), preferred_element_type=F32).astype(BF16)

    w = w_ref[...]
    TH = T // 2
    parts = []

    def logit_copy(h, d, slot):
        return pltpu.make_async_remote_copy(
            src_ref=lmine.at[h], dst_ref=lrecv.at[h, slot], send_sem=l_send.at[h, d], recv_sem=l_recv.at[h, slot],
            device_id={"head": lax.rem(hd + d, H)}, device_id_type=MESH)

    for h in range(2):
        pairs(h * nb // 4, (h + 1) * nb // 4, attend)
        part = lax.dot_general(
            jnp.broadcast_to(w, (16, D)), att_ref[h * half : (h + 1) * half].reshape(TH, D), CONTRACT_LAST,
            preferred_element_type=F32)[0:1]
        lmine[h] = part
        parts.append(part)
        for d in range(1, H):
            logit_copy(h, d, hd).start()
    results[0].start()

    def output_grad(h):
        logits = parts[h]
        for d in range(1, H):
            slot = lax.rem(hd + d, H)
            logit_copy(h, d, slot).wait_recv()
            logits = logits + lrecv[h, slot]
        cols = slice(h * TH, (h + 1) * TH)
        blocks = slice(h * half, (h + 1) * half)
        target = lab_s[:, cols].astype(F32)
        e = jnp.exp(-jnp.abs(logits))
        loss_ref[:, cols] = jnp.maximum(logits, 0.0) + jnp.log1p(e) - target * logits
        sig = jnp.where(logits >= 0, 1.0, e) / (1.0 + e)
        dl = jnp.broadcast_to(sig - target, (8, TH)).T[:, 0:1]
        grad_out = up_s[blocks].reshape(TH, D).astype(F32) + dl * w.astype(F32)
        g_s[blocks] = grad_out.astype(BF16).reshape(half, BLOCK, D)

    def score_grad(i):
        dp = lax.dot_general(g_s[i], gather(vall, i), CONTRACT_LAST, preferred_element_type=F32)
        p = p_s[i]
        rd = jnp.sum(p * dp, axis=-1, keepdims=True)
        ds = p * (dp - rd) * inv
        ds_s[i] = ds.astype(BF16)
        dst_s[pl.ds(i * SLOTS, SLOTS)] = by_slot(ds)

    output_grad(0)
    pairs(0, nb // 4, score_grad)
    output_grad(1)
    results[1].start()

    terms = ((dst_s, q_s, ds_s), (pt_s, g_s, pb_s))

    def slot_term(a, e):
        return jnp.dot(terms[a][0][e], terms[a][1][lax.div(e, jnp.int32(SLOTS))], preferred_element_type=F32)

    def out_copy(a, d, peer, slot):
        return seq_copy(og.at[a, peer], og_in.at[a, slot], o_send.at[a, d], o_recv.at[a, slot], peer)

    def peers(step):
        def one(n, carry):
            d = S - 1 - n
            step(d, xor(me, d, S))
            return carry

        lax.fori_loop(0, S - 1, one, 0)

    def send_random(a):
        def step(d, peer):
            for t in range(cap):
                og[a, peer, t] = slot_term(a, sidx[peer, t]).astype(BF16)
            out_copy(a, d, peer, me).start()

        peers(step)

    is_part = lax.rem(me, stride) == 0
    my_part = lax.div(me, jnp.int32(stride))

    def part_copy(a, j, owner, slot):
        return seq_copy(
            gsend.at[a, pl.ds(j * rows, rows)], grecv.at[a, slot], gp_send.at[a, j], gp_recv.at[a, slot], owner)

    def share_copy(a, d, peer, slot):
        return seq_copy(gsum.at[a], gall.at[a, slot], gb_send.at[a, d], gb_recv.at[a, slot], peer)

    def parts_loop(step):
        def one(t, carry):
            j = lax.rem(my_part + t, PARTS)

            @pl.when(j * stride != me)
            def _():
                step(j)

            return carry

        lax.fori_loop(0, PARTS, one, 0)

    def send_global(a):
        both = terms[a][2][:, :, (3 + RAND) * BLOCK :].reshape(T, GLOBAL * BLOCK)
        gsend[a] = lax.dot_general(
            both, terms[a][1][...].reshape(T, D), CONTRACT_FIRST, preferred_element_type=F32).astype(BF16)
        parts_loop(lambda j: part_copy(a, j, j * stride, me).start())

    def share_global(a):
        @pl.when(is_part)
        def _():
            total = gsend[a, pl.ds(my_part * rows, rows)].astype(F32)
            for d in range(1, S):
                peer = flip(me, d)
                part_copy(a, my_part, peer, peer).wait_recv()
                total = total + grecv[a, peer].astype(F32)
            gsum[a] = total.astype(BF16)
            gall[a, my_part] = gsum[a]
            peers(lambda d, peer: share_copy(a, d, peer, my_part).start())

    prev, following = lax.rem(me + S - 1, S), lax.rem(me + 1, S)

    def edge_copies(a):
        return (
            seq_copy(edge_out.at[a, 0], edge_in.at[a, 1], e_send.at[a, 0], e_recv.at[a, 1], prev),
            seq_copy(edge_out.at[a, 1], edge_in.at[a, 0], e_send.at[a, 1], e_recv.at[a, 0], following),
        )

    def window(a):
        def step(i):
            left = terms[a][0][pl.ds(i * SLOTS, 3)].reshape(WIN, BLOCK)
            acc[a, pl.ds(i, 3)] += jnp.dot(
                left, terms[a][1][i], preferred_element_type=F32).reshape(3, BLOCK, D)

        pairs(0, nb // 2, step)
        edge_out[a, 0] = acc[a, 0].astype(BF16)
        edge_out[a, 1] = acc[a, nb + 1].astype(BF16)
        for copy in edge_copies(a):
            copy.start()

    def take(a, blocks, places):
        for b in range(nb):
            value = acc[a, 1 + b]
            for block, place in zip(blocks, places):
                value = value + block * (place == b).astype(F32)
            acc[a, 1 + b] = value

    def take_own(a):
        take(a, [slot_term(a, sidx[me, t]) for t in range(cap)], [roff[me, t] for t in range(cap)])

    def take_random(a):
        def step(d, peer):
            out_copy(a, d, peer, peer).wait_recv()
            take(a, [og_in[a, peer, t].astype(F32) for t in range(cap)], [roff[peer, t] for t in range(cap)])

        peers(step)

    def take_rest(a):
        for copy in edge_copies(a):
            copy.wait_recv()
        acc[a, 1] += edge_in[a, 0].astype(F32)
        acc[a, nb] += edge_in[a, 1].astype(F32)
        parts_loop(lambda j: share_copy(a, 0, me, j).wait_recv())
        count = PARTS // GLOBAL
        blocks = [
            gall[a, n * count : (n + 1) * count].astype(F32).reshape(BLOCK, D) for n in range(GLOBAL)]
        take(a, blocks, [glob_ref[n] - me * nb for n in range(GLOBAL)])

    send_global(1)
    send_random(1)

    pairs(nb // 4, nb // 2, score_grad)
    share_global(1)
    send_global(0)
    send_random(0)
    window(0)
    window(1)
    share_global(0)

    def grad_q(i):
        dq_ref[i] = jnp.dot(ds_s[i], gather(kall, i), preferred_element_type=F32)

    pairs(0, nb // 2, grad_q)
    results[2].start()
    take_own(1)
    take_own(0)
    take_random(1)
    take_rest(1)
    dv_ref[...] = acc[1, 1 : nb + 1]
    results[4].start()
    take_random(0)
    take_rest(0)
    dk_ref[...] = acc[0, 1 : nb + 1]
    results[3].start()

    for copy in results:
        copy.wait()
    for copy in sends:
        copy.wait_send()
    for h in range(2):
        for d in range(1, H):
            logit_copy(h, d, hd).wait_send()
    for a in range(2):
        peers(lambda d, peer: out_copy(a, d, peer, me).wait_send())
        parts_loop(lambda j: part_copy(a, j, j * stride, me).wait_send())
        for copy in edge_copies(a):
            copy.wait_send()

        @pl.when(is_part)
        def _():
            peers(lambda d, peer: share_copy(a, d, peer, my_part).wait_send())


def store(*refs):
    count = (len(refs) - 2) // 3
    src, dst, buf = (refs[n * count : (n + 1) * count] for n in range(3))
    loads = [pltpu.make_async_copy(src[n], buf[n], refs[-2].at[n]) for n in range(count)]
    stores = [pltpu.make_async_copy(buf[n], dst[n], refs[-1].at[n]) for n in range(count)]
    for copy in loads:
        copy.start()
    for load, copy in zip(loads, stores):
        load.wait()
        copy.start()
    for copy in stores:
        copy.wait()


def body(S, H, queries, key_rows, value_rows, upstream, exit_weight, labels, rand_blocks, glob_blocks):
    T, D = queries.shape
    nb = T // BLOCK
    cap = max(1, (nb * RAND + S - 1) // S)
    rows = GLOBAL * BLOCK // PARTS
    blocked = lambda x: x.reshape(nb, BLOCK, D)
    vmem = pl.BlockSpec(memory_space=pltpu.VMEM)
    smem = pl.BlockSpec(memory_space=pltpu.SMEM)
    hbm = pl.BlockSpec(memory_space=pltpu.HBM)
    dma = pltpu.SemaphoreType.DMA
    results = (
        jax.ShapeDtypeStruct((nb, BLOCK, D), BF16),
        jax.ShapeDtypeStruct((1, T), F32),
        jax.ShapeDtypeStruct((nb, BLOCK, D), F32),
        jax.ShapeDtypeStruct((nb, BLOCK, D), F32),
        jax.ShapeDtypeStruct((nb, BLOCK, D), F32),
    )
    done = pl.pallas_call(
        functools.partial(kernel, S, H, nb, D, cap),
        out_shape=results,
        in_specs=[hbm] * 4 + [vmem, hbm] + [smem] * 2,
        out_specs=[hbm] * 5,
        scratch_shapes=[pltpu.VMEM(x.shape, x.dtype) for x in results] + [
            pltpu.VMEM((1, T), jnp.int32),
            pltpu.VMEM((nb, BLOCK, D), BF16),
            pltpu.VMEM((nb, BLOCK, D), BF16),
            pltpu.VMEM((S * nb, BLOCK, D), BF16),
            pltpu.VMEM((S * nb, BLOCK, D), BF16),
            pltpu.VMEM((nb, BLOCK, SLOTS * BLOCK), F32),
            pltpu.VMEM((nb, BLOCK, SLOTS * BLOCK), BF16),
            pltpu.VMEM((nb * SLOTS, BLOCK, BLOCK), BF16),
            pltpu.VMEM((nb, BLOCK, SLOTS * BLOCK), BF16),
            pltpu.VMEM((nb * SLOTS, BLOCK, BLOCK), BF16),
            pltpu.VMEM((nb, BLOCK, D), BF16),
            pltpu.VMEM((2, S, cap, BLOCK, D), BF16),
            pltpu.VMEM((2, S, cap, BLOCK, D), BF16),
            pltpu.VMEM((2, nb + 2, BLOCK, D), F32),
            pltpu.VMEM((2, GLOBAL * BLOCK, D), BF16),
            pltpu.VMEM((2, S, rows, D), BF16),
            pltpu.VMEM((2, rows, D), BF16),
            pltpu.VMEM((2, PARTS, rows, D), BF16),
            pltpu.VMEM((2, 2, BLOCK, D), BF16),
            pltpu.VMEM((2, 2, BLOCK, D), BF16),
            pltpu.VMEM((2, 1, T // 2), F32),
            pltpu.VMEM((2, H, 1, T // 2), F32),
            pltpu.SMEM((S, cap), jnp.int32),
            pltpu.SMEM((S, cap), jnp.int32),
            dma((5,)),
            dma((2, 2 * S + 2)), dma((2, S, 2)),
            dma((2, H)), dma((2, H)),
            dma((2, S)), dma((2, S)),
            dma((2, 2)), dma((2, 2)),
            dma((2, PARTS)), dma((2, S)),
            dma((2, S)), dma((2, PARTS)), dma((5,)),
        ],
        compiler_params=pltpu.CompilerParams(
            collective_id=0, has_side_effects=True, vmem_limit_bytes=VMEM),
    )(
        blocked(queries), blocked(key_rows), blocked(value_rows), blocked(upstream),
        exit_weight.reshape(1, D), labels.reshape(1, T), rand_blocks.T, glob_blocks,
    )
    att, loss, dq, dk, dv = pl.pallas_call(
        store,
        out_shape=results,
        in_specs=[hbm] * 5,
        out_specs=[hbm] * 5,
        scratch_shapes=[pltpu.VMEM(x.shape, x.dtype) for x in results] + [dma((5,))] * 2,
        compiler_params=pltpu.CompilerParams(vmem_limit_bytes=VMEM),
    )(*done)
    flat = lambda x: x.reshape(T, D)
    return (flat(att), loss.reshape(T), flat(dq), flat(dk), flat(dv))


def solution(mesh):
    placed = (
        P("seq", "head"),
        P("seq", "head"),
        P("seq", "head"),
        P("seq", "head"),
        P("head"),
        P("seq"),
        P(),
        P(),
    )
    return jax.shard_map(
        functools.partial(body, mesh.shape["seq"], mesh.shape["head"]),
        mesh=mesh,
        in_specs=placed,
        out_specs=(
            P("seq", "head"),
            P("seq"),
            P("seq", "head"),
            P("seq", "head"),
            P("seq", "head"),
        ),
        check_vma=False,
    )
```

```python
import functools
import math

import jax
import jax.numpy as jnp
from jax import lax
from jax.experimental import pallas as pl
from jax.experimental.pallas import tpu as pltpu
from jax.sharding import PartitionSpec as P

BLOCK = 64
RAND = 3
GLOBAL = 2
SLOTS = 3 + RAND + GLOBAL
MESH = pl.DeviceIdType.MESH
F32 = jnp.float32
BF16 = jnp.bfloat16
CONTRACT_LAST = (((1,), (1,)), ((), ()))
CONTRACT_FIRST = (((0,), (0,)), ((), ()))
PARTS = 8
VMEM = 63 * 1024 * 1024


def flip(me, bits):
    out = me
    bit = 1
    while bit <= bits:
        if bits & bit:
            out = out + (1 - 2 * lax.rem(lax.div(me, jnp.int32(bit)), jnp.int32(2))) * bit
        bit *= 2
    return out


def kernel(
    S, H, nb, D, cap,
    q_ref, k_ref, v_ref, up_ref, w_ref, lab_ref, rand_ref, glob_ref,
    att_out, loss_out, dq_out, dk_out, dv_out,
    att_ref, loss_ref, dq_ref, dk_ref, dv_ref, lab_s, q_s, up_s, kall, vall, p_s, pb_s, pt_s, ds_s, dst_s, g_s, og, og_in, acc, gsend, grecv, gsum, gall,
    edge_out, edge_in, lmine, lrecv, sidx, roff,
    in_sem, ag_send, ag_recv, l_send, l_recv, o_send, o_recv, e_send, e_recv,
    gp_send, gp_recv, gb_send, gb_recv, out_sem,
):
    me = lax.axis_index("seq")
    hd = lax.axis_index("head")
    N = S * nb
    inv = 1.0 / math.sqrt(D)
    stride = max(1, S // PARTS)
    rows = GLOBAL * BLOCK // PARTS
    T = nb * BLOCK
    half = nb // 2
    WIN = 3 * BLOCK
    mine = pl.ds(me * nb, nb)
    at = [flip(me, d) for d in range(S)]

    def seq_copy(src, dst, ssem, rsem, peer):
        return pltpu.make_async_remote_copy(
            src_ref=src, dst_ref=dst, send_sem=ssem, recv_sem=rsem,
            device_id={"seq": peer}, device_id_type=MESH)

    local = [
        pltpu.make_async_copy(src, dst, in_sem.at[n])
        for n, (src, dst) in enumerate(
            ((k_ref, kall.at[mine]), (v_ref, vall.at[mine]), (q_ref, q_s), (up_ref, up_s), (lab_ref, lab_s)))
    ]
    for copy in local:
        copy.start()
    results = [
        pltpu.make_async_copy(src, dst, out_sem.at[n])
        for n, (src, dst) in enumerate(
            ((att_ref, att_out), (loss_ref, loss_out), (dq_ref, dq_out), (dk_ref, dk_out), (dv_ref, dv_out)))
    ]

    barrier = pltpu.get_barrier_semaphore()
    for d in range(1, S):
        pl.semaphore_signal(barrier, inc=1, device_id={"seq": at[d]}, device_id_type=MESH)
    for d in range(1, H):
        pl.semaphore_signal(barrier, inc=1, device_id={"head": lax.rem(hd + d, H)}, device_id_type=MESH)
    pl.semaphore_wait(barrier, S - 1 + H - 1)

    full = (kall, vall)
    partner = at[1]
    sends = []

    def push(a, n, owner, lo, count, piece, peer):
        part = full[a].at[pl.ds(owner * nb + lo, count)]
        copy = seq_copy(part, part, ag_send.at[a, n], ag_recv.at[a, owner, piece], peer)
        copy.start()
        sends.append(copy)

    def arrived(a, owner, lo, count, piece):
        part = full[a].at[pl.ds(owner * nb + lo, count)]
        seq_copy(part, part, ag_send.at[a, 0], ag_recv.at[a, owner, piece], partner).wait_recv()

    two_step = S == 8
    evens = [2, 4] if two_step else list(range(2, S, 2))

    def own(a):
        for d in evens + [1]:
            push(a, d, me, 0, nb, 0, at[d])

    def relay(a):
        for n, d in enumerate(evens):
            owner = at[d]
            arrived(a, owner, 0, nb, 0)
            if two_step:
                push(a, 8 + n, owner, n * half, half, n, at[6 - d])
            push(a, S + 2 + d, owner, 0, nb, 0, partner)

    def corner(a):
        if two_step:
            owner = at[6]
            for n in range(2):
                arrived(a, owner, n * half, half, n)
                push(a, 5 + 2 * n, owner, n * half, half, n, partner)

    def finish(a):
        for d in range(1, S, 2):
            owner = at[d]
            if two_step and d == 7:
                for n in range(2):
                    arrived(a, owner, n * half, half, n)
            else:
                arrived(a, owner, 0, nb, 0)

    for a in range(2):
        local[a].wait()
        own(a)

    def tables(s, carry):
        cnt, cnt2 = jnp.int32(0), jnp.int32(0)
        idx = [jnp.int32(3)] * cap
        off = [jnp.int32(-1)] * cap
        for j in range(nb * RAND):
            b = rand_ref[j % RAND, me * nb + j // RAND] - s * nb
            hit = (b >= 0) & (b < nb)
            place = rand_ref[j % RAND, s * nb + j // RAND] - me * nb
            hit2 = (place >= 0) & (place < nb)
            for t in range(cap):
                idx[t] = jnp.where(hit & (cnt == t), j // RAND * SLOTS + 3 + j % RAND, idx[t])
                off[t] = jnp.where(hit2 & (cnt2 == t), place, off[t])
            cnt = cnt + hit.astype(jnp.int32)
            cnt2 = cnt2 + hit2.astype(jnp.int32)
        for t in range(cap):
            sidx[s, t] = idx[t]
            roff[s, t] = off[t]
        return carry

    lax.fori_loop(0, S, tables, 0)
    acc[...] = jnp.zeros_like(acc)

    relay(0)
    relay(1)
    corner(0)
    finish(0)
    for copy in local[2:]:
        copy.wait()

    def gather(all_ref, i):
        gi = me * nb + i
        ids = [lax.rem(gi + N - 1, N), gi, lax.rem(gi + 1, N)]
        ids += [rand_ref[r, gi] for r in range(RAND)]
        ids += [glob_ref[r] for r in range(GLOBAL)]
        return jnp.concatenate([all_ref[b] for b in ids], axis=0)

    def by_slot(x):
        return x.T.astype(BF16).reshape(SLOTS, BLOCK, BLOCK)

    def pairs(lo, hi, step):
        for i in range(2 * lo, 2 * hi):
            step(i)

    col = lax.broadcasted_iota(jnp.int32, (BLOCK, SLOTS * BLOCK), 1)

    def softmax(i):
        keys = gather(kall, i)
        s = lax.dot_general(q_s[i], keys, CONTRACT_LAST, preferred_element_type=F32) * inv
        gi = me * nb + i
        low = jnp.where(gi == 0, BLOCK, 0)
        void = (col < low) | ((col >= 2 * BLOCK) & (col < jnp.where(gi == N - 1, 3 * BLOCK, 0)))
        s = jnp.where(void, -jnp.inf, s)
        e = jnp.exp(s - jnp.max(s, axis=-1, keepdims=True))
        p = e * (1.0 / jnp.sum(e, axis=-1, keepdims=True))
        p_s[i] = p
        pb_s[i] = p.astype(BF16)
        pt_s[pl.ds(i * SLOTS, SLOTS)] = by_slot(p)

    pairs(0, nb // 4, softmax)
    corner(1)
    pairs(nb // 4, nb // 2, softmax)
    finish(1)

    def attend(i):
        att_ref[i] = jnp.dot(pb_s[i], gather(vall, i), preferred_element_type=F32).astype(BF16)

    w = w_ref[...]
    TH = T // 2
    parts = []

    def logit_copy(h, d, slot):
        return pltpu.make_async_remote_copy(
            src_ref=lmine.at[h], dst_ref=lrecv.at[h, slot], send_sem=l_send.at[h, d], recv_sem=l_recv.at[h, slot],
            device_id={"head": lax.rem(hd + d, H)}, device_id_type=MESH)

    for h in range(2):
        pairs(h * nb // 4, (h + 1) * nb // 4, attend)
        part = lax.dot_general(
            jnp.broadcast_to(w, (16, D)), att_ref[h * half : (h + 1) * half].reshape(TH, D), CONTRACT_LAST,
            preferred_element_type=F32)[0:1]
        lmine[h] = part
        parts.append(part)
        for d in range(1, H):
            logit_copy(h, d, hd).start()
    results[0].start()

    def output_grad(h):
        logits = parts[h]
        for d in range(1, H):
            slot = lax.rem(hd + d, H)
            logit_copy(h, d, slot).wait_recv()
            logits = logits + lrecv[h, slot]
        cols = slice(h * TH, (h + 1) * TH)
        blocks = slice(h * half, (h + 1) * half)
        target = lab_s[:, cols].astype(F32)
        e = jnp.exp(-jnp.abs(logits))
        loss_ref[:, cols] = jnp.maximum(logits, 0.0) + jnp.log1p(e) - target * logits
        sig = jnp.where(logits >= 0, 1.0, e) / (1.0 + e)
        dl = jnp.broadcast_to(sig - target, (8, TH)).T[:, 0:1]
        grad_out = up_s[blocks].reshape(TH, D).astype(F32) + dl * w.astype(F32)
        g_s[blocks] = grad_out.astype(BF16).reshape(half, BLOCK, D)

    def score_grad(i):
        dp = lax.dot_general(g_s[i], gather(vall, i), CONTRACT_LAST, preferred_element_type=F32)
        p = p_s[i]
        rd = jnp.sum(p * dp, axis=-1, keepdims=True)
        ds = p * (dp - rd) * inv
        ds_s[i] = ds.astype(BF16)
        dst_s[pl.ds(i * SLOTS, SLOTS)] = by_slot(ds)

    output_grad(0)
    pairs(0, nb // 4, score_grad)
    output_grad(1)
    results[1].start()

    terms = ((dst_s, q_s, ds_s), (pt_s, g_s, pb_s))

    def slot_term(a, e):
        return jnp.dot(terms[a][0][e], terms[a][1][lax.div(e, jnp.int32(SLOTS))], preferred_element_type=F32)

    def out_copy(a, d, peer, slot):
        return seq_copy(og.at[a, peer], og_in.at[a, slot], o_send.at[a, d], o_recv.at[a, slot], peer)

    def peers(step):
        for d in range(S - 1, 0, -1):
            step(d, at[d])

    def send_random(a):
        def step(d, peer):
            for t in range(cap):
                og[a, peer, t] = slot_term(a, sidx[peer, t]).astype(BF16)
            out_copy(a, d, peer, me).start()

        peers(step)

    on_part = (lambda f: f()) if stride == 1 else pl.when(lax.rem(me, stride) == 0)
    my_part = lax.div(me, jnp.int32(stride))

    def part_copy(a, j, owner, slot):
        return seq_copy(
            gsend.at[a, pl.ds(j * rows, rows)], grecv.at[a, slot], gp_send.at[a, j], gp_recv.at[a, slot], owner)

    def share_copy(a, d, peer, slot):
        return seq_copy(gsum.at[a], gall.at[a, slot], gb_send.at[a, d], gb_recv.at[a, slot], peer)

    def parts_loop(step):
        for t in range(1 if stride == 1 else 0, PARTS):
            j = lax.rem(my_part + t, PARTS)
            if stride == 1:
                step(j)
            else:
                pl.when(j * stride != me)(functools.partial(step, j))

    def send_global(a):
        both = terms[a][2][:, :, (3 + RAND) * BLOCK :].reshape(T, GLOBAL * BLOCK)
        gsend[a] = lax.dot_general(
            both, terms[a][1][...].reshape(T, D), CONTRACT_FIRST, preferred_element_type=F32).astype(BF16)
        parts_loop(lambda j: part_copy(a, j, j * stride, me).start())

    def share_global(a):
        @on_part
        def _():
            total = gsend[a, pl.ds(my_part * rows, rows)].astype(F32)
            for d in range(1, S):
                peer = at[d]
                part_copy(a, my_part, peer, peer).wait_recv()
                total = total + grecv[a, peer].astype(F32)
            gsum[a] = total.astype(BF16)
            gall[a, my_part] = gsum[a]
            peers(lambda d, peer: share_copy(a, d, peer, my_part).start())

    prev, following = lax.rem(me + S - 1, S), lax.rem(me + 1, S)

    def edge_copies(a):
        return (
            seq_copy(edge_out.at[a, 0], edge_in.at[a, 1], e_send.at[a, 0], e_recv.at[a, 1], prev),
            seq_copy(edge_out.at[a, 1], edge_in.at[a, 0], e_send.at[a, 1], e_recv.at[a, 0], following),
        )

    def window(a):
        def step(i):
            left = terms[a][0][pl.ds(i * SLOTS, 3)].reshape(WIN, BLOCK)
            acc[a, pl.ds(i, 3)] += jnp.dot(
                left, terms[a][1][i], preferred_element_type=F32).reshape(3, BLOCK, D)

        pairs(0, nb // 2, step)
        edge_out[a, 0] = acc[a, 0].astype(BF16)
        edge_out[a, 1] = acc[a, nb + 1].astype(BF16)
        for copy in edge_copies(a):
            copy.start()

    def take(a, blocks, places):
        for b in range(nb):
            value = acc[a, 1 + b]
            for block, place in zip(blocks, places):
                value = value + block * (place == b).astype(F32)
            acc[a, 1 + b] = value

    def take_own(a):
        take(a, [slot_term(a, sidx[me, t]) for t in range(cap)], [roff[me, t] for t in range(cap)])

    def take_random(a):
        def step(d, peer):
            out_copy(a, d, peer, peer).wait_recv()
            take(a, [og_in[a, peer, t].astype(F32) for t in range(cap)], [roff[peer, t] for t in range(cap)])

        peers(step)

    def take_rest(a):
        for copy in edge_copies(a):
            copy.wait_recv()
        acc[a, 1] += edge_in[a, 0].astype(F32)
        acc[a, nb] += edge_in[a, 1].astype(F32)
        parts_loop(lambda j: share_copy(a, 0, me, j).wait_recv())
        count = PARTS // GLOBAL
        blocks = [
            gall[a, n * count : (n + 1) * count].astype(F32).reshape(BLOCK, D) for n in range(GLOBAL)]
        take(a, blocks, [glob_ref[n] - me * nb for n in range(GLOBAL)])

    send_global(1)
    send_random(1)

    pairs(nb // 4, nb // 2, score_grad)
    share_global(1)
    send_global(0)
    send_random(0)
    window(0)
    window(1)
    share_global(0)

    def grad_q(i):
        dq_ref[i] = jnp.dot(ds_s[i], gather(kall, i), preferred_element_type=F32)

    pairs(0, nb // 2, grad_q)
    results[2].start()
    take_own(1)
    take_own(0)
    take_random(1)
    take_rest(1)
    dv_ref[...] = acc[1, 1 : nb + 1]
    results[4].start()
    take_random(0)
    take_rest(0)
    dk_ref[...] = acc[0, 1 : nb + 1]
    results[3].start()

    for copy in sends:
        copy.wait_send()
    for h in range(2):
        for d in range(1, H):
            logit_copy(h, d, hd).wait_send()
    for a in range(2):
        peers(lambda d, peer: out_copy(a, d, peer, me).wait_send())
        parts_loop(lambda j: part_copy(a, j, j * stride, me).wait_send())
        for copy in edge_copies(a):
            copy.wait_send()

        @on_part
        def _():
            peers(lambda d, peer: share_copy(a, d, peer, my_part).wait_send())
    for copy in results:
        copy.wait()


def store(*refs):
    count = (len(refs) - 2) // 3
    src, dst, buf = (refs[n * count : (n + 1) * count] for n in range(3))
    loads = [pltpu.make_async_copy(src[n], buf[n], refs[-2].at[n]) for n in range(count)]
    stores = [pltpu.make_async_copy(buf[n], dst[n], refs[-1].at[n]) for n in range(count)]
    for copy in loads:
        copy.start()
    for load, copy in zip(loads, stores):
        load.wait()
        copy.start()
    for copy in stores:
        copy.wait()


def body(S, H, queries, key_rows, value_rows, upstream, exit_weight, labels, rand_blocks, glob_blocks):
    T, D = queries.shape
    nb = T // BLOCK
    cap = max(1, (nb * RAND + S - 1) // S)
    rows = GLOBAL * BLOCK // PARTS
    blocked = lambda x: x.reshape(nb, BLOCK, D)
    vmem = pl.BlockSpec(memory_space=pltpu.VMEM)
    smem = pl.BlockSpec(memory_space=pltpu.SMEM)
    hbm = pl.BlockSpec(memory_space=pltpu.HBM)
    dma = pltpu.SemaphoreType.DMA
    results = (
        jax.ShapeDtypeStruct((nb, BLOCK, D), BF16),
        jax.ShapeDtypeStruct((1, T), F32),
        jax.ShapeDtypeStruct((nb, BLOCK, D), F32),
        jax.ShapeDtypeStruct((nb, BLOCK, D), F32),
        jax.ShapeDtypeStruct((nb, BLOCK, D), F32),
    )
    done = pl.pallas_call(
        functools.partial(kernel, S, H, nb, D, cap),
        out_shape=results,
        in_specs=[hbm] * 4 + [vmem, hbm] + [smem] * 2,
        out_specs=[hbm] * 5,
        scratch_shapes=[pltpu.VMEM(x.shape, x.dtype) for x in results] + [
            pltpu.VMEM((1, T), jnp.int32),
            pltpu.VMEM((nb, BLOCK, D), BF16),
            pltpu.VMEM((nb, BLOCK, D), BF16),
            pltpu.VMEM((S * nb, BLOCK, D), BF16),
            pltpu.VMEM((S * nb, BLOCK, D), BF16),
            pltpu.VMEM((nb, BLOCK, SLOTS * BLOCK), F32),
            pltpu.VMEM((nb, BLOCK, SLOTS * BLOCK), BF16),
            pltpu.VMEM((nb * SLOTS, BLOCK, BLOCK), BF16),
            pltpu.VMEM((nb, BLOCK, SLOTS * BLOCK), BF16),
            pltpu.VMEM((nb * SLOTS, BLOCK, BLOCK), BF16),
            pltpu.VMEM((nb, BLOCK, D), BF16),
            pltpu.VMEM((2, S, cap, BLOCK, D), BF16),
            pltpu.VMEM((2, S, cap, BLOCK, D), BF16),
            pltpu.VMEM((2, nb + 2, BLOCK, D), F32),
            pltpu.VMEM((2, GLOBAL * BLOCK, D), BF16),
            pltpu.VMEM((2, S, rows, D), BF16),
            pltpu.VMEM((2, rows, D), BF16),
            pltpu.VMEM((2, PARTS, rows, D), BF16),
            pltpu.VMEM((2, 2, BLOCK, D), BF16),
            pltpu.VMEM((2, 2, BLOCK, D), BF16),
            pltpu.VMEM((2, 1, T // 2), F32),
            pltpu.VMEM((2, H, 1, T // 2), F32),
            pltpu.SMEM((S, cap), jnp.int32),
            pltpu.SMEM((S, cap), jnp.int32),
            dma((5,)),
            dma((2, 2 * S + 2)), dma((2, S, 2)),
            dma((2, H)), dma((2, H)),
            dma((2, S)), dma((2, S)),
            dma((2, 2)), dma((2, 2)),
            dma((2, PARTS)), dma((2, S)),
            dma((2, S)), dma((2, PARTS)), dma((5,)),
        ],
        compiler_params=pltpu.CompilerParams(
            collective_id=0, has_side_effects=True, vmem_limit_bytes=VMEM),
    )(
        blocked(queries), blocked(key_rows), blocked(value_rows), blocked(upstream),
        exit_weight.reshape(1, D), labels.reshape(1, T), rand_blocks.T, glob_blocks,
    )
    att, loss, dq, dk, dv = pl.pallas_call(
        store,
        out_shape=results,
        in_specs=[hbm] * 5,
        out_specs=[hbm] * 5,
        scratch_shapes=[pltpu.VMEM(x.shape, x.dtype) for x in results] + [dma((5,))] * 2,
        compiler_params=pltpu.CompilerParams(vmem_limit_bytes=VMEM),
    )(*done)
    flat = lambda x: x.reshape(T, D)
    return (flat(att), loss.reshape(T), flat(dq), flat(dk), flat(dv))


def solution(mesh):
    placed = (
        P("seq", "head"),
        P("seq", "head"),
        P("seq", "head"),
        P("seq", "head"),
        P("head"),
        P("seq"),
        P(),
        P(),
    )
    return jax.shard_map(
        functools.partial(body, mesh.shape["seq"], mesh.shape["head"]),
        mesh=mesh,
        in_specs=placed,
        out_specs=(
            P("seq", "head"),
            P("seq"),
            P("seq", "head"),
            P("seq", "head"),
            P("seq", "head"),
        ),
        check_vma=False,
    )
```

```python
import functools
import math

import jax
import jax.numpy as jnp
from jax import lax
from jax.experimental import pallas as pl
from jax.experimental.pallas import tpu as pltpu
from jax.sharding import PartitionSpec as P

BLOCK = 64
RAND = 3
GLOBAL = 2
SLOTS = 3 + RAND + GLOBAL
MESH = pl.DeviceIdType.MESH
F32 = jnp.float32
BF16 = jnp.bfloat16
CONTRACT_LAST = (((1,), (1,)), ((), ()))
CONTRACT_FIRST = (((0,), (0,)), ((), ()))
PARTS = 8
VMEM = 63 * 1024 * 1024


def flip(me, bits):
    out = me
    bit = 1
    while bit <= bits:
        if bits & bit:
            out = out + (1 - 2 * lax.rem(lax.div(me, jnp.int32(bit)), jnp.int32(2))) * bit
        bit *= 2
    return out


def kernel(
    S, H, nb, D, cap,
    q_ref, k_ref, v_ref, up_ref, w_ref, lab_ref, rand_ref, glob_ref,
    att_out, loss_out, dq_out, dk_out, dv_out,
    att_ref, loss_ref, dq_ref, dk_ref, dv_ref, lab_s, q_s, up_s, kall, vall, p_s, pb_s, pt_s, ds_s, dst_s, g_s, og, og_in, acc, gsend, grecv, gsum, gall,
    edge_out, edge_in, lmine, lrecv, sidx, roff,
    in_sem, ag_send, ag_recv, l_send, l_recv, o_send, o_recv, e_send, e_recv,
    gp_send, gp_recv, gb_send, gb_recv, out_sem,
):
    me = lax.axis_index("seq")
    hd = lax.axis_index("head")
    N = S * nb
    inv = 1.0 / math.sqrt(D)
    stride = max(1, S // PARTS)
    rows = GLOBAL * BLOCK // PARTS
    T = nb * BLOCK
    half = nb // 2
    WIN = 3 * BLOCK
    mine = pl.ds(me * nb, nb)
    at = [flip(me, d) for d in range(S)]

    def seq_copy(src, dst, ssem, rsem, peer):
        return pltpu.make_async_remote_copy(
            src_ref=src, dst_ref=dst, send_sem=ssem, recv_sem=rsem,
            device_id={"seq": peer}, device_id_type=MESH)

    local = [
        pltpu.make_async_copy(src, dst, in_sem.at[n])
        for n, (src, dst) in enumerate(
            ((k_ref, kall.at[mine]), (v_ref, vall.at[mine]), (q_ref, q_s), (up_ref, up_s), (lab_ref, lab_s)))
    ]
    for copy in local:
        copy.start()
    results = [
        pltpu.make_async_copy(src, dst, out_sem.at[n])
        for n, (src, dst) in enumerate(
            ((att_ref, att_out), (loss_ref, loss_out), (dq_ref, dq_out), (dk_ref, dk_out), (dv_ref, dv_out)))
    ]

    barrier = pltpu.get_barrier_semaphore()
    for d in range(1, S):
        pl.semaphore_signal(barrier, inc=1, device_id={"seq": at[d]}, device_id_type=MESH)
    for d in range(1, H):
        pl.semaphore_signal(barrier, inc=1, device_id={"head": lax.rem(hd + d, H)}, device_id_type=MESH)
    pl.semaphore_wait(barrier, S - 1 + H - 1)

    full = (kall, vall)
    partner = at[1]
    sends = []

    def push(a, n, owner, lo, count, piece, peer):
        part = full[a].at[pl.ds(owner * nb + lo, count)]
        copy = seq_copy(part, part, ag_send.at[a, n], ag_recv.at[a, owner, piece], peer)
        copy.start()
        sends.append(copy)

    def arrived(a, owner, lo, count, piece):
        part = full[a].at[pl.ds(owner * nb + lo, count)]
        seq_copy(part, part, ag_send.at[a, 0], ag_recv.at[a, owner, piece], partner).wait_recv()

    two_step = S == 8
    evens = [2, 4] if two_step else list(range(2, S, 2))

    def own(a):
        for d in evens + [1]:
            push(a, d, me, 0, nb, 0, at[d])

    def relay(a):
        for n, d in enumerate(evens):
            owner = at[d]
            arrived(a, owner, 0, nb, 0)
            if two_step:
                push(a, 8 + n, owner, n * half, half, n, at[6 - d])
            push(a, S + 2 + d, owner, 0, nb, 0, partner)

    def corner(a):
        if two_step:
            owner = at[6]
            for n in range(2):
                arrived(a, owner, n * half, half, n)
                push(a, 5 + 2 * n, owner, n * half, half, n, partner)

    def finish(a):
        for d in range(1, S, 2):
            owner = at[d]
            if two_step and d == 7:
                for n in range(2):
                    arrived(a, owner, n * half, half, n)
            else:
                arrived(a, owner, 0, nb, 0)

    for a in range(2):
        local[a].wait()
        own(a)

    def tables(s, carry):
        cnt, cnt2 = jnp.int32(0), jnp.int32(0)
        idx = [jnp.int32(3)] * cap
        off = [jnp.int32(-1)] * cap
        for j in range(nb * RAND):
            b = rand_ref[j % RAND, me * nb + j // RAND] - s * nb
            hit = (b >= 0) & (b < nb)
            place = rand_ref[j % RAND, s * nb + j // RAND] - me * nb
            hit2 = (place >= 0) & (place < nb)
            for t in range(cap):
                idx[t] = jnp.where(hit & (cnt == t), j // RAND * SLOTS + 3 + j % RAND, idx[t])
                off[t] = jnp.where(hit2 & (cnt2 == t), place, off[t])
            cnt = cnt + hit.astype(jnp.int32)
            cnt2 = cnt2 + hit2.astype(jnp.int32)
        for t in range(cap):
            sidx[s, t] = idx[t]
            roff[s, t] = off[t]
        return carry

    lax.fori_loop(0, S, tables, 0)
    acc[...] = jnp.zeros_like(acc)

    relay(0)
    relay(1)
    corner(0)
    finish(0)
    for copy in local[2:]:
        copy.wait()

    def gather(all_ref, i):
        gi = me * nb + i
        ids = [lax.rem(gi + N - 1, N), gi, lax.rem(gi + 1, N)]
        ids += [rand_ref[r, gi] for r in range(RAND)]
        ids += [glob_ref[r] for r in range(GLOBAL)]
        return jnp.concatenate([all_ref[b] for b in ids], axis=0)

    def by_slot(x):
        return x.T.astype(BF16).reshape(SLOTS, BLOCK, BLOCK)

    def pairs(lo, hi, step):
        for i in range(2 * lo, 2 * hi):
            step(i)

    col = lax.broadcasted_iota(jnp.int32, (BLOCK, SLOTS * BLOCK), 1)

    def softmax(i):
        keys = gather(kall, i)
        s = lax.dot_general(q_s[i], keys, CONTRACT_LAST, preferred_element_type=F32) * inv
        gi = me * nb + i
        low = jnp.where(gi == 0, BLOCK, 0)
        void = (col < low) | ((col >= 2 * BLOCK) & (col < jnp.where(gi == N - 1, 3 * BLOCK, 0)))
        s = jnp.where(void, -jnp.inf, s)
        e = jnp.exp(s - jnp.max(s, axis=-1, keepdims=True))
        p = e * (1.0 / jnp.sum(e, axis=-1, keepdims=True))
        p_s[i] = p
        pb_s[i] = p.astype(BF16)
        pt_s[pl.ds(i * SLOTS, SLOTS)] = by_slot(p)

    pairs(0, nb // 4, softmax)
    corner(1)
    pairs(nb // 4, nb // 2, softmax)
    finish(1)

    def attend(i):
        att_ref[i] = jnp.dot(pb_s[i], gather(vall, i), preferred_element_type=F32).astype(BF16)

    w = w_ref[...]
    TH = T // 2
    parts = []

    def logit_copy(h, d, slot):
        return pltpu.make_async_remote_copy(
            src_ref=lmine.at[h], dst_ref=lrecv.at[h, slot], send_sem=l_send.at[h, d], recv_sem=l_recv.at[h, slot],
            device_id={"head": lax.rem(hd + d, H)}, device_id_type=MESH)

    for h in range(2):
        pairs(h * nb // 4, (h + 1) * nb // 4, attend)
        part = lax.dot_general(
            jnp.broadcast_to(w, (16, D)), att_ref[h * half : (h + 1) * half].reshape(TH, D), CONTRACT_LAST,
            preferred_element_type=F32)[0:1]
        lmine[h] = part
        parts.append(part)
        for d in range(1, H):
            logit_copy(h, d, hd).start()
    results[0].start()

    def output_grad(h):
        logits = parts[h]
        for d in range(1, H):
            slot = lax.rem(hd + d, H)
            logit_copy(h, d, slot).wait_recv()
            logits = logits + lrecv[h, slot]
        cols = slice(h * TH, (h + 1) * TH)
        blocks = slice(h * half, (h + 1) * half)
        target = lab_s[:, cols].astype(F32)
        e = jnp.exp(-jnp.abs(logits))
        loss_ref[:, cols] = jnp.maximum(logits, 0.0) + jnp.log1p(e) - target * logits
        sig = jnp.where(logits >= 0, 1.0, e) / (1.0 + e)
        dl = jnp.broadcast_to(sig - target, (8, TH)).T[:, 0:1]
        grad_out = up_s[blocks].reshape(TH, D).astype(F32) + dl * w.astype(F32)
        g_s[blocks] = grad_out.astype(BF16).reshape(half, BLOCK, D)

    def score_grad(i):
        dp = lax.dot_general(g_s[i], gather(vall, i), CONTRACT_LAST, preferred_element_type=F32)
        p = p_s[i]
        rd = jnp.sum(p * dp, axis=-1, keepdims=True)
        ds = p * (dp - rd) * inv
        ds_s[i] = ds.astype(BF16)
        dst_s[pl.ds(i * SLOTS, SLOTS)] = by_slot(ds)

    output_grad(0)
    output_grad(1)
    results[1].start()

    terms = ((dst_s, q_s, ds_s), (pt_s, g_s, pb_s))

    def slot_term(a, e):
        return jnp.dot(terms[a][0][e], terms[a][1][lax.div(e, jnp.int32(SLOTS))], preferred_element_type=F32)

    def out_copy(a, d, peer, slot):
        return seq_copy(og.at[a, peer], og_in.at[a, slot], o_send.at[a, d], o_recv.at[a, slot], peer)

    order = [6, 4, 2, 7, 5, 3, 1] if two_step else list(range(S - 1, 0, -1))

    def peers(step):
        for d in order:
            step(d, at[d])

    def send_random(a):
        def step(d, peer):
            for t in range(cap):
                og[a, peer, t] = slot_term(a, sidx[peer, t]).astype(BF16)
            out_copy(a, d, peer, me).start()

        peers(step)

    on_part = (lambda f: f()) if stride == 1 else pl.when(lax.rem(me, stride) == 0)
    my_part = lax.div(me, jnp.int32(stride))

    def part_copy(j, owner, slot):
        return seq_copy(gsend.at[j], grecv.at[slot], gp_send.at[j], gp_recv.at[slot], owner)

    def share_copy(d, peer, slot):
        return seq_copy(gsum, gall.at[slot], gb_send.at[d], gb_recv.at[slot], peer)

    def parts_loop(step):
        for t in range(1 if stride == 1 else 0, PARTS):
            j = lax.rem(my_part + t, PARTS)
            if stride == 1:
                step(j)
            else:
                pl.when(j * stride != me)(functools.partial(step, j))

    def send_global():
        for a in range(2):
            both = terms[a][2][:, :, (3 + RAND) * BLOCK :].reshape(T, GLOBAL * BLOCK)
            gsend[:, a] = lax.dot_general(
                both, terms[a][1][...].reshape(T, D), CONTRACT_FIRST, preferred_element_type=F32
            ).astype(BF16).reshape(PARTS, rows, D)
        parts_loop(lambda j: part_copy(j, j * stride, me).start())

    def share_global():
        @on_part
        def _():
            total = gsend[my_part].astype(F32)
            for d in range(1, S):
                part_copy(my_part, at[d], at[d]).wait_recv()
                total = total + grecv[at[d]].astype(F32)
            gsum[...] = total.astype(BF16)
            gall[my_part] = gsum[...]
            peers(lambda d, peer: share_copy(d, peer, my_part).start())

    prev, following = lax.rem(me + S - 1, S), lax.rem(me + 1, S)

    def edge_copies(a):
        return (
            seq_copy(edge_out.at[a, 0], edge_in.at[a, 1], e_send.at[a, 0], e_recv.at[a, 1], prev),
            seq_copy(edge_out.at[a, 1], edge_in.at[a, 0], e_send.at[a, 1], e_recv.at[a, 0], following),
        )

    def window(a):
        def step(i):
            left = terms[a][0][pl.ds(i * SLOTS, 3)].reshape(WIN, BLOCK)
            acc[a, pl.ds(i, 3)] += jnp.dot(
                left, terms[a][1][i], preferred_element_type=F32).reshape(3, BLOCK, D)

        pairs(0, nb // 2, step)
        edge_out[a, 0] = acc[a, 0].astype(BF16)
        edge_out[a, 1] = acc[a, nb + 1].astype(BF16)
        for copy in edge_copies(a):
            copy.start()

    def take(a, blocks, places):
        for b in range(nb):
            value = acc[a, 1 + b]
            for block, place in zip(blocks, places):
                value = value + block * (place == b).astype(F32)
            acc[a, 1 + b] = value

    def take_own(a):
        take(a, [slot_term(a, sidx[me, t]) for t in range(cap)], [roff[me, t] for t in range(cap)])

    def take_random(a):
        def step(d, peer):
            out_copy(a, d, peer, peer).wait_recv()
            take(a, [og_in[a, peer, t].astype(F32) for t in range(cap)], [roff[peer, t] for t in range(cap)])

        peers(step)

    def take_rest(a):
        for copy in edge_copies(a):
            copy.wait_recv()
        acc[a, 1] += edge_in[a, 0].astype(F32)
        acc[a, nb] += edge_in[a, 1].astype(F32)
        count = PARTS // GLOBAL
        blocks = [
            gall[n * count : (n + 1) * count, a].astype(F32).reshape(BLOCK, D) for n in range(GLOBAL)]
        take(a, blocks, [glob_ref[n] - me * nb for n in range(GLOBAL)])

    send_random(1)
    pairs(0, nb // 2, score_grad)
    send_global()
    send_random(0)
    window(0)
    window(1)
    share_global()

    def grad_q(i):
        dq_ref[i] = jnp.dot(ds_s[i], gather(kall, i), preferred_element_type=F32)

    pairs(0, nb // 2, grad_q)
    results[2].start()
    take_own(1)
    take_own(0)
    take_random(1)
    parts_loop(lambda j: share_copy(0, me, j).wait_recv())
    take_rest(1)
    dv_ref[...] = acc[1, 1 : nb + 1]
    results[4].start()
    take_random(0)
    take_rest(0)
    dk_ref[...] = acc[0, 1 : nb + 1]
    results[3].start()

    for copy in sends:
        copy.wait_send()
    for h in range(2):
        for d in range(1, H):
            logit_copy(h, d, hd).wait_send()
    for a in range(2):
        peers(lambda d, peer: out_copy(a, d, peer, me).wait_send())
        for copy in edge_copies(a):
            copy.wait_send()

    parts_loop(lambda j: part_copy(j, j * stride, me).wait_send())

    @on_part
    def _():
        peers(lambda d, peer: share_copy(d, peer, my_part).wait_send())

    for copy in results:
        copy.wait()


def store(*refs):
    count = (len(refs) - 2) // 3
    src, dst, buf = (refs[n * count : (n + 1) * count] for n in range(3))
    loads = [pltpu.make_async_copy(src[n], buf[n], refs[-2].at[n]) for n in range(count)]
    stores = [pltpu.make_async_copy(buf[n], dst[n], refs[-1].at[n]) for n in range(count)]
    for copy in loads:
        copy.start()
    for load, copy in zip(loads, stores):
        load.wait()
        copy.start()
    for copy in stores:
        copy.wait()


def body(S, H, queries, key_rows, value_rows, upstream, exit_weight, labels, rand_blocks, glob_blocks):
    T, D = queries.shape
    nb = T // BLOCK
    cap = max(1, (nb * RAND + S - 1) // S)
    rows = GLOBAL * BLOCK // PARTS
    blocked = lambda x: x.reshape(nb, BLOCK, D)
    vmem = pl.BlockSpec(memory_space=pltpu.VMEM)
    smem = pl.BlockSpec(memory_space=pltpu.SMEM)
    hbm = pl.BlockSpec(memory_space=pltpu.HBM)
    dma = pltpu.SemaphoreType.DMA
    results = (
        jax.ShapeDtypeStruct((nb, BLOCK, D), BF16),
        jax.ShapeDtypeStruct((1, T), F32),
        jax.ShapeDtypeStruct((nb, BLOCK, D), F32),
        jax.ShapeDtypeStruct((nb, BLOCK, D), F32),
        jax.ShapeDtypeStruct((nb, BLOCK, D), F32),
    )
    done = pl.pallas_call(
        functools.partial(kernel, S, H, nb, D, cap),
        out_shape=results,
        in_specs=[hbm] * 4 + [vmem, hbm] + [smem] * 2,
        out_specs=[hbm] * 5,
        scratch_shapes=[pltpu.VMEM(x.shape, x.dtype) for x in results] + [
            pltpu.VMEM((1, T), jnp.int32),
            pltpu.VMEM((nb, BLOCK, D), BF16),
            pltpu.VMEM((nb, BLOCK, D), BF16),
            pltpu.VMEM((S * nb, BLOCK, D), BF16),
            pltpu.VMEM((S * nb, BLOCK, D), BF16),
            pltpu.VMEM((nb, BLOCK, SLOTS * BLOCK), F32),
            pltpu.VMEM((nb, BLOCK, SLOTS * BLOCK), BF16),
            pltpu.VMEM((nb * SLOTS, BLOCK, BLOCK), BF16),
            pltpu.VMEM((nb, BLOCK, SLOTS * BLOCK), BF16),
            pltpu.VMEM((nb * SLOTS, BLOCK, BLOCK), BF16),
            pltpu.VMEM((nb, BLOCK, D), BF16),
            pltpu.VMEM((2, S, cap, BLOCK, D), BF16),
            pltpu.VMEM((2, S, cap, BLOCK, D), BF16),
            pltpu.VMEM((2, nb + 2, BLOCK, D), F32),
            pltpu.VMEM((PARTS, 2, rows, D), BF16),
            pltpu.VMEM((S, 2, rows, D), BF16),
            pltpu.VMEM((2, rows, D), BF16),
            pltpu.VMEM((PARTS, 2, rows, D), BF16),
            pltpu.VMEM((2, 2, BLOCK, D), BF16),
            pltpu.VMEM((2, 2, BLOCK, D), BF16),
            pltpu.VMEM((2, 1, T // 2), F32),
            pltpu.VMEM((2, H, 1, T // 2), F32),
            pltpu.SMEM((S, cap), jnp.int32),
            pltpu.SMEM((S, cap), jnp.int32),
            dma((5,)),
            dma((2, 2 * S + 2)), dma((2, S, 2)),
            dma((2, H)), dma((2, H)),
            dma((2, S)), dma((2, S)),
            dma((2, 2)), dma((2, 2)),
            dma((PARTS,)), dma((S,)),
            dma((S,)), dma((PARTS,)), dma((5,)),
        ],
        compiler_params=pltpu.CompilerParams(
            collective_id=0, has_side_effects=True, vmem_limit_bytes=VMEM),
    )(
        blocked(queries), blocked(key_rows), blocked(value_rows), blocked(upstream),
        exit_weight.reshape(1, D), labels.reshape(1, T), rand_blocks.T, glob_blocks,
    )
    att, loss, dq, dk, dv = pl.pallas_call(
        store,
        out_shape=results,
        in_specs=[hbm] * 5,
        out_specs=[hbm] * 5,
        scratch_shapes=[pltpu.VMEM(x.shape, x.dtype) for x in results] + [dma((5,))] * 2,
        compiler_params=pltpu.CompilerParams(vmem_limit_bytes=VMEM),
    )(*done)
    flat = lambda x: x.reshape(T, D)
    return (flat(att), loss.reshape(T), flat(dq), flat(dk), flat(dv))


def solution(mesh):
    placed = (
        P("seq", "head"),
        P("seq", "head"),
        P("seq", "head"),
        P("seq", "head"),
        P("head"),
        P("seq"),
        P(),
        P(),
    )
    return jax.shard_map(
        functools.partial(body, mesh.shape["seq"], mesh.shape["head"]),
        mesh=mesh,
        in_specs=placed,
        out_specs=(
            P("seq", "head"),
            P("seq"),
            P("seq", "head"),
            P("seq", "head"),
            P("seq", "head"),
        ),
        check_vma=False,
    )
```

```python
import functools
import math

import jax
import jax.numpy as jnp
from jax import lax
from jax.experimental import pallas as pl
from jax.experimental.pallas import tpu as pltpu
from jax.sharding import PartitionSpec as P

BLOCK = 64
RAND = 3
GLOBAL = 2
SLOTS = 3 + RAND + GLOBAL
MESH = pl.DeviceIdType.MESH
F32 = jnp.float32
BF16 = jnp.bfloat16
CONTRACT_LAST = (((1,), (1,)), ((), ()))
CONTRACT_FIRST = (((0,), (0,)), ((), ()))
PARTS = 8
VMEM = 63 * 1024 * 1024


def flip(me, bits):
    out = me
    bit = 1
    while bit <= bits:
        if bits & bit:
            out = out + (1 - 2 * lax.rem(lax.div(me, jnp.int32(bit)), jnp.int32(2))) * bit
        bit *= 2
    return out


def kernel(
    S, H, nb, D, cap,
    q_ref, k_ref, v_ref, up_ref, w_ref, lab_ref, rand_ref, glob_ref,
    att_out, loss_out, dq_out, dk_out, dv_out,
    att_ref, loss_ref, dq_ref, dk_ref, dv_ref, lab_s, q_s, up_s, kall, vall, p_s, pb_s, pt_s, ds_s, dst_s, g_s, og, og_in, acc, gsend, grecv, gsum, gall,
    edge_out, edge_in, lmine, lrecv, sidx, roff,
    in_sem, ag_send, ag_recv, l_send, l_recv, o_send, o_recv, e_send, e_recv,
    gp_send, gp_recv, gb_send, gb_recv, out_sem, dlr_s, cs, cs_in, c_send, c_recv,
):
    me = lax.axis_index("seq")
    hd = lax.axis_index("head")
    N = S * nb
    inv = 1.0 / math.sqrt(D)
    stride = max(1, S // PARTS)
    rows = GLOBAL * BLOCK // PARTS
    T = nb * BLOCK
    half = nb // 2
    WIN = 3 * BLOCK
    mine = pl.ds(me * nb, nb)
    at = [flip(me, d) for d in range(S)]

    def seq_copy(src, dst, ssem, rsem, peer):
        return pltpu.make_async_remote_copy(
            src_ref=src, dst_ref=dst, send_sem=ssem, recv_sem=rsem,
            device_id={"seq": peer}, device_id_type=MESH)

    local = [
        pltpu.make_async_copy(src, dst, in_sem.at[n])
        for n, (src, dst) in enumerate(
            ((k_ref, kall.at[mine]), (v_ref, vall.at[mine]), (q_ref, q_s), (up_ref, up_s), (lab_ref, lab_s)))
    ]
    for copy in local:
        copy.start()
    results = [
        pltpu.make_async_copy(src, dst, out_sem.at[n])
        for n, (src, dst) in enumerate(
            ((att_ref, att_out), (loss_ref, loss_out), (dq_ref, dq_out), (dk_ref, dk_out), (dv_ref, dv_out)))
    ]

    barrier = pltpu.get_barrier_semaphore()
    for d in range(1, S):
        pl.semaphore_signal(barrier, inc=1, device_id={"seq": at[d]}, device_id_type=MESH)
    for d in range(1, H):
        pl.semaphore_signal(barrier, inc=1, device_id={"head": lax.rem(hd + d, H)}, device_id_type=MESH)
    pl.semaphore_wait(barrier, S - 1 + H - 1)

    full = (kall, vall)
    partner = at[1]
    sends = []

    def push(a, n, owner, lo, count, piece, peer):
        part = full[a].at[pl.ds(owner * nb + lo, count)]
        copy = seq_copy(part, part, ag_send.at[a, n], ag_recv.at[a, owner, piece], peer)
        copy.start()
        sends.append(copy)

    def arrived(a, owner, lo, count, piece):
        part = full[a].at[pl.ds(owner * nb + lo, count)]
        seq_copy(part, part, ag_send.at[a, 0], ag_recv.at[a, owner, piece], partner).wait_recv()

    two_step = S == 8
    evens = [2, 4] if two_step else list(range(2, S, 2))

    def own(a):
        for d in evens + [1]:
            push(a, d, me, 0, nb, 0, at[d])

    def relay(a):
        for n, d in enumerate(evens):
            owner = at[d]
            arrived(a, owner, 0, nb, 0)
            if two_step:
                push(a, 8 + n, owner, n * half, half, n, at[6 - d])
            push(a, S + 2 + d, owner, 0, nb, 0, partner)

    def corner(a):
        if two_step:
            owner = at[6]
            for n in range(2):
                arrived(a, owner, n * half, half, n)
                push(a, 5 + 2 * n, owner, n * half, half, n, partner)

    def finish(a):
        for d in range(1, S, 2):
            owner = at[d]
            if two_step and d == 7:
                for n in range(2):
                    arrived(a, owner, n * half, half, n)
            else:
                arrived(a, owner, 0, nb, 0)

    for a in range(2):
        local[a].wait()
        own(a)

    def tables(s, carry):
        cnt, cnt2 = jnp.int32(0), jnp.int32(0)
        idx = [jnp.int32(3)] * cap
        off = [jnp.int32(-1)] * cap
        for j in range(nb * RAND):
            b = rand_ref[j % RAND, me * nb + j // RAND] - s * nb
            hit = (b >= 0) & (b < nb)
            place = rand_ref[j % RAND, s * nb + j // RAND] - me * nb
            hit2 = (place >= 0) & (place < nb)
            for t in range(cap):
                idx[t] = jnp.where(hit & (cnt == t), j // RAND * SLOTS + 3 + j % RAND, idx[t])
                off[t] = jnp.where(hit2 & (cnt2 == t), place, off[t])
            cnt = cnt + hit.astype(jnp.int32)
            cnt2 = cnt2 + hit2.astype(jnp.int32)
        for t in range(cap):
            sidx[s, t] = idx[t]
            roff[s, t] = off[t]
        return carry

    lax.fori_loop(0, S, tables, 0)
    acc[...] = jnp.zeros_like(acc)

    relay(0)
    relay(1)
    corner(0)
    finish(0)
    for copy in local[2:]:
        copy.wait()

    def gather(all_ref, i):
        gi = me * nb + i
        ids = [lax.rem(gi + N - 1, N), gi, lax.rem(gi + 1, N)]
        ids += [rand_ref[r, gi] for r in range(RAND)]
        ids += [glob_ref[r] for r in range(GLOBAL)]
        return jnp.concatenate([all_ref[b] for b in ids], axis=0)

    def by_slot(x):
        return x.T.astype(BF16).reshape(SLOTS, BLOCK, BLOCK)

    def pairs(lo, hi, step):
        for i in range(2 * lo, 2 * hi):
            step(i)

    col = lax.broadcasted_iota(jnp.int32, (BLOCK, SLOTS * BLOCK), 1)

    def softmax(i):
        keys = gather(kall, i)
        s = lax.dot_general(q_s[i], keys, CONTRACT_LAST, preferred_element_type=F32) * inv
        gi = me * nb + i
        low = jnp.where(gi == 0, BLOCK, 0)
        void = (col < low) | ((col >= 2 * BLOCK) & (col < jnp.where(gi == N - 1, 3 * BLOCK, 0)))
        s = jnp.where(void, -jnp.inf, s)
        e = jnp.exp(s - jnp.max(s, axis=-1, keepdims=True))
        p = e * (1.0 / jnp.sum(e, axis=-1, keepdims=True))
        p_s[i] = p
        pb_s[i] = p.astype(BF16)
        pt_s[pl.ds(i * SLOTS, SLOTS)] = by_slot(p)

    pairs(0, nb // 4, softmax)
    corner(1)
    pairs(nb // 4, nb // 2, softmax)
    terms = ((dst_s, q_s, ds_s), (pt_s, g_s, pb_s))

    def slot_term(a, e, right=None):
        right = terms[a][1] if right is None else right
        return jnp.dot(terms[a][0][e], right[lax.div(e, jnp.int32(SLOTS))], preferred_element_type=F32)

    def out_copy(a, d, peer, slot):
        return seq_copy(og.at[a, peer], og_in.at[a, slot], o_send.at[a, d], o_recv.at[a, slot], peer)

    order = [6, 4, 2, 7, 5, 3, 1] if two_step else list(range(S - 1, 0, -1))

    def peers(step):
        for d in order:
            step(d, at[d])

    def send_random(a, right=None):
        def step(d, peer):
            for t in range(cap):
                og[a, peer, t] = slot_term(a, sidx[peer, t], right).astype(BF16)
            out_copy(a, d, peer, me).start()

        peers(step)

    row = lax.broadcasted_iota(jnp.int32, (16, BLOCK), 0)

    def corr_copy(d, peer, slot):
        return seq_copy(cs.at[peer], cs_in.at[slot], c_send.at[d], c_recv.at[slot], peer)

    def two_rows(x, t, row=row):
        high = x.astype(BF16).astype(F32)
        return jnp.where(row == 2 * t, high, jnp.where(row == 2 * t + 1, x - high, 0.0))

    def send_corrections():
        def step(d, peer):
            rows16 = jnp.zeros((16, BLOCK), F32)
            for t in range(cap):
                e = sidx[peer, t]
                r = lax.dot_general(
                    dlr_s[lax.div(e, jnp.int32(SLOTS))], pt_s[e], CONTRACT_LAST, preferred_element_type=F32)
                rows16 = rows16 + two_rows(r[0:1] + r[1:2], t)
            cs[peer] = jnp.concatenate([rows16, jnp.zeros_like(rows16)], axis=1).astype(BF16)
            corr_copy(d, peer, me).start()

        peers(step)

    def correction(peer, t):
        x = cs_in[peer][:, :BLOCK].astype(F32)
        x = jnp.where((row >= 2 * t) & (row < 2 * t + 2), x, 0.0).astype(BF16)
        return lax.dot_general(
            x, jnp.broadcast_to(w_ref[...], (16, D)), CONTRACT_FIRST, preferred_element_type=F32)

    send_random(1, up_s)

    finish(1)

    def attend(i):
        att_ref[i] = jnp.dot(pb_s[i], gather(vall, i), preferred_element_type=F32).astype(BF16)

    w = w_ref[...]
    TH = T // 2
    parts = []

    def logit_copy(h, d, slot):
        return pltpu.make_async_remote_copy(
            src_ref=lmine.at[h], dst_ref=lrecv.at[h, slot], send_sem=l_send.at[h, d], recv_sem=l_recv.at[h, slot],
            device_id={"head": lax.rem(hd + d, H)}, device_id_type=MESH)

    for h in range(2):
        pairs(h * nb // 4, (h + 1) * nb // 4, attend)
        part = lax.dot_general(
            jnp.broadcast_to(w, (16, D)), att_ref[h * half : (h + 1) * half].reshape(TH, D), CONTRACT_LAST,
            preferred_element_type=F32)[0:1]
        lmine[h] = part
        parts.append(part)
        for d in range(1, H):
            logit_copy(h, d, hd).start()
    results[0].start()

    def output_grad(h):
        logits = parts[h]
        for d in range(1, H):
            slot = lax.rem(hd + d, H)
            logit_copy(h, d, slot).wait_recv()
            logits = logits + lrecv[h, slot]
        cols = slice(h * TH, (h + 1) * TH)
        blocks = slice(h * half, (h + 1) * half)
        target = lab_s[:, cols].astype(F32)
        e = jnp.exp(-jnp.abs(logits))
        loss_ref[:, cols] = jnp.maximum(logits, 0.0) + jnp.log1p(e) - target * logits
        sig = jnp.where(logits >= 0, 1.0, e) / (1.0 + e)
        dl = jnp.broadcast_to(sig - target, (8, TH)).T[:, 0:1]
        grad_out = up_s[blocks].reshape(TH, D).astype(F32) + dl * w.astype(F32)
        rows16 = two_rows(sig - target, 0, lax.broadcasted_iota(jnp.int32, (16, TH), 0)).astype(BF16)
        for b in range(half):
            dlr_s[h * half + b] = rows16[:, b * BLOCK : (b + 1) * BLOCK]
        g_s[blocks] = grad_out.astype(BF16).reshape(half, BLOCK, D)

    def score_grad(i):
        dp = lax.dot_general(g_s[i], gather(vall, i), CONTRACT_LAST, preferred_element_type=F32)
        p = p_s[i]
        rd = jnp.sum(p * dp, axis=-1, keepdims=True)
        ds = p * (dp - rd) * inv
        ds_s[i] = ds.astype(BF16)
        dst_s[pl.ds(i * SLOTS, SLOTS)] = by_slot(ds)

    output_grad(0)
    output_grad(1)
    results[1].start()

    on_part = (lambda f: f()) if stride == 1 else pl.when(lax.rem(me, stride) == 0)
    my_part = lax.div(me, jnp.int32(stride))

    def part_copy(j, owner, slot):
        return seq_copy(gsend.at[j], grecv.at[slot], gp_send.at[j], gp_recv.at[slot], owner)

    def share_copy(d, peer, slot):
        return seq_copy(gsum, gall.at[slot], gb_send.at[d], gb_recv.at[slot], peer)

    def parts_loop(step):
        for t in range(1 if stride == 1 else 0, PARTS):
            j = lax.rem(my_part + t, PARTS)
            if stride == 1:
                step(j)
            else:
                pl.when(j * stride != me)(functools.partial(step, j))

    def send_global():
        for a in range(2):
            both = terms[a][2][:, :, (3 + RAND) * BLOCK :].reshape(T, GLOBAL * BLOCK)
            gsend[:, a] = lax.dot_general(
                both, terms[a][1][...].reshape(T, D), CONTRACT_FIRST, preferred_element_type=F32
            ).astype(BF16).reshape(PARTS, rows, D)
        parts_loop(lambda j: part_copy(j, j * stride, me).start())

    def share_global():
        @on_part
        def _():
            total = gsend[my_part].astype(F32)
            for d in range(1, S):
                part_copy(my_part, at[d], at[d]).wait_recv()
                total = total + grecv[at[d]].astype(F32)
            gsum[...] = total.astype(BF16)
            gall[my_part] = gsum[...]
            peers(lambda d, peer: share_copy(d, peer, my_part).start())

    prev, following = lax.rem(me + S - 1, S), lax.rem(me + 1, S)

    def edge_copies(a):
        return (
            seq_copy(edge_out.at[a, 0], edge_in.at[a, 1], e_send.at[a, 0], e_recv.at[a, 1], prev),
            seq_copy(edge_out.at[a, 1], edge_in.at[a, 0], e_send.at[a, 1], e_recv.at[a, 0], following),
        )

    def window(a):
        def step(i):
            left = terms[a][0][pl.ds(i * SLOTS, 3)].reshape(WIN, BLOCK)
            acc[a, pl.ds(i, 3)] += jnp.dot(
                left, terms[a][1][i], preferred_element_type=F32).reshape(3, BLOCK, D)

        pairs(0, nb // 2, step)
        edge_out[a, 0] = acc[a, 0].astype(BF16)
        edge_out[a, 1] = acc[a, nb + 1].astype(BF16)
        for copy in edge_copies(a):
            copy.start()

    def take(a, blocks, places):
        for b in range(nb):
            value = acc[a, 1 + b]
            for block, place in zip(blocks, places):
                value = value + block * (place == b).astype(F32)
            acc[a, 1 + b] = value

    def take_own(a):
        take(a, [slot_term(a, sidx[me, t]) for t in range(cap)], [roff[me, t] for t in range(cap)])

    def take_random(a):
        def step(d, peer):
            out_copy(a, d, peer, peer).wait_recv()
            blocks = [og_in[a, peer, t].astype(F32) for t in range(cap)]
            if a == 1:
                corr_copy(d, peer, peer).wait_recv()
                blocks = [x + correction(peer, t) for t, x in enumerate(blocks)]
            take(a, blocks, [roff[peer, t] for t in range(cap)])

        peers(step)

    def take_rest(a):
        for copy in edge_copies(a):
            copy.wait_recv()
        acc[a, 1] += edge_in[a, 0].astype(F32)
        acc[a, nb] += edge_in[a, 1].astype(F32)
        count = PARTS // GLOBAL
        blocks = [
            gall[n * count : (n + 1) * count, a].astype(F32).reshape(BLOCK, D) for n in range(GLOBAL)]
        take(a, blocks, [glob_ref[n] - me * nb for n in range(GLOBAL)])

    send_corrections()
    pairs(0, nb // 2, score_grad)
    send_global()
    send_random(0)
    window(0)
    window(1)
    share_global()

    def grad_q(i):
        dq_ref[i] = jnp.dot(ds_s[i], gather(kall, i), preferred_element_type=F32)

    pairs(0, nb // 2, grad_q)
    results[2].start()
    take_own(1)
    take_own(0)
    take_random(1)
    parts_loop(lambda j: share_copy(0, me, j).wait_recv())
    take_rest(1)
    dv_ref[...] = acc[1, 1 : nb + 1]
    results[4].start()
    take_random(0)
    take_rest(0)
    dk_ref[...] = acc[0, 1 : nb + 1]
    results[3].start()

    for copy in sends:
        copy.wait_send()
    for h in range(2):
        for d in range(1, H):
            logit_copy(h, d, hd).wait_send()
    for a in range(2):
        peers(lambda d, peer: out_copy(a, d, peer, me).wait_send())
        for copy in edge_copies(a):
            copy.wait_send()

    parts_loop(lambda j: part_copy(j, j * stride, me).wait_send())
    peers(lambda d, peer: corr_copy(d, peer, me).wait_send())

    @on_part
    def _():
        peers(lambda d, peer: share_copy(d, peer, my_part).wait_send())

    for copy in results:
        copy.wait()


def store(*refs):
    count = (len(refs) - 2) // 3
    src, dst, buf = (refs[n * count : (n + 1) * count] for n in range(3))
    loads, stores = [], []
    for n in range(count):
        lead = src[n].shape[0]
        pieces = 4 if lead % 4 == 0 else 1
        for piece in range(pieces):
            cut = pl.ds(piece * (lead // pieces), lead // pieces)
            loads.append(pltpu.make_async_copy(src[n].at[cut], buf[n].at[cut], refs[-2].at[n, piece]))
            stores.append(pltpu.make_async_copy(buf[n].at[cut], dst[n].at[cut], refs[-1].at[n, piece]))
    for copy in loads:
        copy.start()
    for load, copy in zip(loads, stores):
        load.wait()
        copy.start()
    for copy in stores:
        copy.wait()


def body(S, H, queries, key_rows, value_rows, upstream, exit_weight, labels, rand_blocks, glob_blocks):
    T, D = queries.shape
    nb = T // BLOCK
    cap = max(1, (nb * RAND + S - 1) // S)
    rows = GLOBAL * BLOCK // PARTS
    blocked = lambda x: x.reshape(nb, BLOCK, D)
    vmem = pl.BlockSpec(memory_space=pltpu.VMEM)
    smem = pl.BlockSpec(memory_space=pltpu.SMEM)
    hbm = pl.BlockSpec(memory_space=pltpu.HBM)
    dma = pltpu.SemaphoreType.DMA
    results = (
        jax.ShapeDtypeStruct((nb, BLOCK, D), BF16),
        jax.ShapeDtypeStruct((1, T), F32),
        jax.ShapeDtypeStruct((nb, BLOCK, D), F32),
        jax.ShapeDtypeStruct((nb, BLOCK, D), F32),
        jax.ShapeDtypeStruct((nb, BLOCK, D), F32),
    )
    done = pl.pallas_call(
        functools.partial(kernel, S, H, nb, D, cap),
        out_shape=results,
        in_specs=[hbm] * 4 + [vmem, hbm] + [smem] * 2,
        out_specs=[hbm] * 5,
        scratch_shapes=[pltpu.VMEM(x.shape, x.dtype) for x in results] + [
            pltpu.VMEM((1, T), jnp.int32),
            pltpu.VMEM((nb, BLOCK, D), BF16),
            pltpu.VMEM((nb, BLOCK, D), BF16),
            pltpu.VMEM((S * nb, BLOCK, D), BF16),
            pltpu.VMEM((S * nb, BLOCK, D), BF16),
            pltpu.VMEM((nb, BLOCK, SLOTS * BLOCK), F32),
            pltpu.VMEM((nb, BLOCK, SLOTS * BLOCK), BF16),
            pltpu.VMEM((nb * SLOTS, BLOCK, BLOCK), BF16),
            pltpu.VMEM((nb, BLOCK, SLOTS * BLOCK), BF16),
            pltpu.VMEM((nb * SLOTS, BLOCK, BLOCK), BF16),
            pltpu.VMEM((nb, BLOCK, D), BF16),
            pltpu.VMEM((2, S, cap, BLOCK, D), BF16),
            pltpu.VMEM((2, S, cap, BLOCK, D), BF16),
            pltpu.VMEM((2, nb + 2, BLOCK, D), F32),
            pltpu.VMEM((PARTS, 2, rows, D), BF16),
            pltpu.VMEM((S, 2, rows, D), BF16),
            pltpu.VMEM((2, rows, D), BF16),
            pltpu.VMEM((PARTS, 2, rows, D), BF16),
            pltpu.VMEM((2, 2, BLOCK, D), BF16),
            pltpu.VMEM((2, 2, BLOCK, D), BF16),
            pltpu.VMEM((2, 1, T // 2), F32),
            pltpu.VMEM((2, H, 1, T // 2), F32),
            pltpu.SMEM((S, cap), jnp.int32),
            pltpu.SMEM((S, cap), jnp.int32),
            dma((5,)),
            dma((2, 2 * S + 2)), dma((2, S, 2)),
            dma((2, H)), dma((2, H)),
            dma((2, S)), dma((2, S)),
            dma((2, 2)), dma((2, 2)),
            dma((PARTS,)), dma((S,)),
            dma((S,)), dma((PARTS,)), dma((5,)),
            pltpu.VMEM((nb, 16, BLOCK), BF16),
            pltpu.VMEM((S, 16, D), BF16),
            pltpu.VMEM((S, 16, D), BF16),
            dma((S,)), dma((S,)),
        ],
        compiler_params=pltpu.CompilerParams(
            collective_id=0, has_side_effects=True, vmem_limit_bytes=VMEM),
    )(
        blocked(queries), blocked(key_rows), blocked(value_rows), blocked(upstream),
        exit_weight.reshape(1, D), labels.reshape(1, T), rand_blocks.T, glob_blocks,
    )
    att, loss, dq, dk, dv = pl.pallas_call(
        store,
        out_shape=results,
        in_specs=[hbm] * 5,
        out_specs=[hbm] * 5,
        scratch_shapes=[pltpu.VMEM(x.shape, x.dtype) for x in results] + [dma((5, 4))] * 2,
        compiler_params=pltpu.CompilerParams(vmem_limit_bytes=VMEM),
    )(*done)
    flat = lambda x: x.reshape(T, D)
    return (flat(att), loss.reshape(T), flat(dq), flat(dk), flat(dv))


def solution(mesh):
    placed = (
        P("seq", "head"),
        P("seq", "head"),
        P("seq", "head"),
        P("seq", "head"),
        P("head"),
        P("seq"),
        P(),
        P(),
    )
    return jax.shard_map(
        functools.partial(body, mesh.shape["seq"], mesh.shape["head"]),
        mesh=mesh,
        in_specs=placed,
        out_specs=(
            P("seq", "head"),
            P("seq"),
            P("seq", "head"),
            P("seq", "head"),
            P("seq", "head"),
        ),
        check_vma=False,
    )
```
